32 devices in a mesh: parts: 2 (over x), store: 16 (over z, y, core).
Axes of the slice: x: 2, y: 2, z: 4, core: 2. Of those that a mesh axis runs over, the one named last changes fastest.
Arguments:
- queries: bfloat16 [8, 8, 64, 128], P(None, 'parts'), parts along dimension 1, may hold values from -6 to 6
- new_keys: bfloat16 [8, 8, 8, 128], P(None, 'parts'), parts along dimension 1, may hold values from -30 to 30
- new_values: bfloat16 [8, 8, 8, 128], P(None, 'parts'), parts along dimension 1, may hold values from -6 to 6
- key_factors: bfloat16 [8, 8192, 160], P('parts', 'store'), parts along dimension 0, may hold values from -6 to 6
- key_basis: bfloat16 [8, 160, 1024], P('parts'), parts along dimension 0, may hold values from -0.5 to 0.5
- values: bfloat16 [8, 8192, 1024], P('parts', 'store'), parts along dimension 0, may hold values from -6 to 6
- block_index: int32 [8, 8, 8, 64], P(None, 'parts'), parts along dimension 1, may hold values from 0 to 1023, as said below
- block_count: int32 [8, 8, 8], P(None, 'parts'), parts along dimension 1, may hold values from 4 to 64
- out_weight: bfloat16 [8192, 8192], P('store'), may hold values from -0.75 to 0.75
Outputs:
- attn_out: bfloat16 [8, 8, 8192], P(None, 'parts', 'store'), parts along dimension 1
The draws below stay inside these ranges and needn't reach their ends.
There are 2 independent parts, one for each index of `parts`. The reference program is written for one: setup_inputs(seed, part) draws one part's arguments, and reference() takes and returns one part's arrays. A program takes and returns all parts, laid end to end along the dimension named above; an argument that names none is the same for every part. Nothing has to cross between parts.
Inputs may be any that keep to these rules, and one draw needn't show every extreme that they name: `block_index`: each list holds 64 distinct block numbers; block c covers tokens 8 c to 8 c + 7. Entries at or past block_count are padding and are ignored. Among the valid entries of one list at most 4 blocks lie in the tokens of one store shard, and in every list some shard holds exactly 4 of them.
All inputs are finite; a program needn't handle non-finite values.
Results may differ from the reference program's by a relative error of at most 0.012.
The reference program's roundings to bfloat16 on the way (of `q_rot`, `new_rot`, `key` and `attn`) count: a program that leaves them out, or rounds other values in their place, can miss the bound.
Values may be sent and summed in bfloat16 or wider, within the bound.
A program may use at most 128 MiB of HBM per device.

```python
import math
import jax
import jax.numpy as jnp
from jax import lax

D = 8192
H = 64
KVH = 8
HD = 128
RANK = 160
BLOCK = 8
MOST = 4
STEPS = 8
REQS = 4
TOK_DEV = 512
KTOP = 64
LENGTH = 8192
N_STORE = 16


def query_base(key):
    normal_part = jnp.clip(jax.random.normal(key, (STEPS, REQS, H, HD), jnp.float32), -4.0, 4.0)
    return normal_part


def draw_queries(key, part):
    return query_base(key).astype(jnp.bfloat16)


def drawn_keys(key, strength_lo, strength_step):
    queries_full = query_base(key)
    noise_key = jax.random.fold_in(key, 7)
    noise = jax.random.normal(noise_key, (STEPS, REQS, KVH, HD), jnp.float32)
    aligned = queries_full[:, :, ::H // KVH]
    strength = strength_lo + strength_step * jnp.arange(REQS, dtype=jnp.float32)
    return jnp.clip(strength[None, :, None, None] * aligned + 0.5 * noise, -30.0, 30.0)


def draw_new_keys(key, part):
    return drawn_keys(key, 0.5, 0.0).astype(jnp.bfloat16)


def draw_block_index(key, part):
    key = jax.random.fold_in(key, 11)
    key_hot, key_start, key_score = jax.random.split(key, 3)
    lists = STEPS * REQS * KVH
    per_shard = TOK_DEV // BLOCK
    stride = per_shard // MOST
    hot_shard = N_STORE - 1 - jax.random.randint(key_hot, (lists,), 0, min(4, N_STORE))
    starts = jax.random.randint(key_start, (lists, N_STORE), 0, per_shard)
    local_ids = (starts[:, :, None] + jnp.arange(MOST, dtype=jnp.int32)[None, None, :] * stride) % per_shard
    global_ids = jnp.arange(N_STORE, dtype=jnp.int32)[None, :, None] * per_shard + local_ids
    hot_rows = jnp.take_along_axis(global_ids, hot_shard[:, None, None], axis=1)[:, 0]
    candidates = global_ids.reshape(lists, N_STORE * MOST)
    shard_of = jnp.repeat(jnp.arange(N_STORE, dtype=jnp.int32), MOST)
    scores = jax.random.randint(key_score, (lists, N_STORE * MOST), 0, 2 ** 20) + shard_of[None, :] * (2 ** 20 // N_STORE)
    scores = jnp.where(shard_of[None, :] == hot_shard[:, None], -1, scores)
    scores = scores * (N_STORE * MOST) + jnp.arange(N_STORE * MOST, dtype=jnp.int32)[None, :]
    unused, picked = lax.top_k(scores, KTOP - MOST)
    rest_rows = jnp.take_along_axis(candidates, picked, axis=1)
    full_rows = jnp.concatenate([hot_rows, rest_rows], axis=1)
    return full_rows.reshape(STEPS, REQS, KVH, KTOP).astype(jnp.int32)


def draw_block_count(key, part):
    key = jax.random.fold_in(key, 12)
    key_count, key_high, key_low = jax.random.split(key, 3)
    lists = STEPS * REQS * KVH
    spans = 1 + (KTOP - MOST) * (jnp.arange(REQS, dtype=jnp.int32) + 1) // REQS
    counts = KTOP - jax.random.randint(key_count, (STEPS, REQS, KVH), 0, spans[None, :, None])
    high_at = jax.random.randint(key_high, (), 0, lists)
    low_at = (high_at + 1 + jax.random.randint(key_low, (), 0, lists - 1)) % lists
    counts = counts.reshape(lists).at[high_at].set(KTOP).at[low_at].set(MOST)
    return counts.reshape(STEPS, REQS, KVH).astype(jnp.int32)


def strengthened(drawn, stream_key, source, target, blocks, factor):
    owner, partner = [(jnp.arange(drawn.shape[position]) // (drawn.shape[position] // blocks)).reshape([-1 if axis == position else 1 for axis in range(drawn.ndim)]) for position in (source, target)]
    chosen = jax.random.permutation(stream_key, blocks)[partner]
    strong = (owner == chosen) | (owner == (partner + blocks // 2) % blocks)
    return jnp.where(strong, factor * drawn, drawn)


def steps_of(rng, shape, cuts, least, top_value):
    def one(axis_at, blocks):
        draws = jax.random.uniform(jax.random.fold_in(jax.random.fold_in(rng, 6), axis_at), (blocks,), jnp.float32, least / len(cuts), top_value / len(cuts))
        return jnp.repeat(jnp.exp(draws), shape[axis_at] // blocks).reshape((-1,) + (1,) * (len(shape) - axis_at - 1))

    gain = one(*cuts[0])
    for cut in cuts[1:]:
        gain = gain * one(*cut)
    return gain


def scatter_about(rng, shape, scale, reach, pieces=(), kind=jnp.bfloat16):
    gain = steps_of(rng, shape, pieces, -0.22, 0.18) if pieces else 1.0
    array = jax.random.normal(rng, shape, jnp.float32) * scale * gain
    return jnp.minimum(jnp.maximum(array, -reach), reach).astype(kind)


def bell_draw_with(rng, extent, spread, reach, shards, heavy, kind=jnp.bfloat16):
    drawn = spread * jax.random.normal(rng, extent, jnp.float32)
    if shards:
        drawn = drawn * steps_of(rng, extent, shards, -0.22, 0.18)
    return jnp.clip(strengthened(drawn, jax.random.fold_in(rng, 3), *heavy), -reach, reach).astype(kind)


def setup_inputs(seed: int = 0, part: int = 0) -> dict:
    splits = jax.random.split(jax.random.key(seed), 10)
    part_splits = jax.random.split(jax.random.fold_in(splits[9], part), 10)
    queries = draw_queries(jax.random.fold_in(jax.random.fold_in(splits[9], part), 71), part)
    new_keys = draw_new_keys(jax.random.fold_in(jax.random.fold_in(splits[9], part), 71), part)
    new_values = scatter_about(part_splits[2], (STEPS, REQS, KVH, HD), 1.0, 6.0)
    key_factors = scatter_about(part_splits[3], (REQS, LENGTH, RANK), 1.0, 6.0, ((1, 16),))
    key_basis = scatter_about(part_splits[4], (REQS, RANK, KVH * HD), RANK ** -0.5, 0.5)
    values = scatter_about(part_splits[5], (REQS, LENGTH, KVH * HD), 1.0, 6.0, ((1, 16),))
    block_index = draw_block_index(jax.random.fold_in(jax.random.fold_in(splits[9], part), 71), part)
    block_count = draw_block_count(jax.random.fold_in(jax.random.fold_in(splits[9], part), 71), part)
    out_weight = bell_draw_with(splits[8], (H * HD, D), HD ** -0.5, 0.75, ((0, 16),), (0, 1, 16, 2.0))
    return dict(queries=queries, new_keys=new_keys, new_values=new_values, key_factors=key_factors, key_basis=key_basis, values=values, block_index=block_index, block_count=block_count, out_weight=out_weight)


ROPE_THETA = 500000.0
NEG_FLOOR = -1e30


def rope_table(head_dim):
    half_dim = head_dim // 2
    exponent = jnp.arange(half_dim, dtype=jnp.float32) * (2.0 / head_dim)
    base_freq = jnp.power(jnp.float32(ROPE_THETA), -exponent)
    wavelength = 2.0 * math.pi / base_freq
    smooth = (8192.0 / wavelength - 1.0) / 3.0
    middle = (1.0 - smooth) * base_freq / 8.0 + smooth * base_freq
    return jnp.where(wavelength < 2048.0, base_freq, jnp.where(wavelength > 8192.0, base_freq / 8.0, middle))


def rotate(vectors, positions, inv_freq):
    angles = positions[..., None] * inv_freq
    cosine = jnp.cos(angles)
    sine_part = jnp.sin(angles)
    half_dim = vectors.shape[-1] // 2
    front_half = vectors[..., :half_dim]
    back_half = vectors[..., half_dim:]
    return jnp.concatenate([front_half * cosine - back_half * sine_part, back_half * cosine + front_half * sine_part], axis=-1)


def softmax_terms(scores, keep_mask, fresh_scores, fresh_mask):
    row_top = jnp.maximum(jnp.max(jnp.where(keep_mask, scores, NEG_FLOOR), axis=-1), jnp.max(jnp.where(fresh_mask, fresh_scores, NEG_FLOOR), axis=-1))
    weights = jnp.where(keep_mask, jnp.exp(scores - row_top[..., None]), 0.0)
    fresh_weights = jnp.where(fresh_mask, jnp.exp(fresh_scores - row_top[..., None]), 0.0)
    return row_top, weights, fresh_weights


def reference(queries, new_keys, new_values, key_factors, key_basis, values, block_index, block_count, out_weight):
    length = key_factors.shape[1]
    group_size = H // KVH
    score_scale = HD ** -0.5
    inv_freq = rope_table(HD)
    step_ids = jnp.arange(STEPS, dtype=jnp.int32)
    step_pos = (length + step_ids).astype(jnp.float32)
    q_rot = rotate(queries.astype(jnp.float32), step_pos[:, None, None], inv_freq).astype(jnp.bfloat16)
    new_rot = rotate(new_keys.astype(jnp.float32), step_pos[:, None, None], inv_freq).astype(jnp.bfloat16)
    basis = key_basis.reshape(REQS, RANK, KVH, HD)
    offsets = jnp.arange(BLOCK, dtype=jnp.int32)
    slot_ids = jnp.arange(KTOP, dtype=jnp.int32)

    def one_list(list_id):
        step_id = list_id // (REQS * KVH)
        request = (list_id // KVH) % REQS
        head_id = list_id % KVH
        tokens = (block_index[step_id, request, head_id][:, None] * BLOCK + offsets).reshape(-1).astype(jnp.int32)
        valid_mask = jnp.repeat(slot_ids < block_count[step_id, request, head_id], BLOCK)
        key_rows = jnp.dot(key_factors[request, tokens], basis[request, :, head_id], preferred_element_type=jnp.float32)
        key_rows = rotate(key_rows, tokens.astype(jnp.float32), inv_freq).astype(jnp.bfloat16)
        value_rows = lax.dynamic_slice_in_dim(values[request, tokens], head_id * HD, HD, 1)
        query_rows = lax.dynamic_slice_in_dim(q_rot[step_id, request], head_id * group_size, group_size, 0)
        scores = jnp.dot(query_rows, key_rows.T, preferred_element_type=jnp.float32) * score_scale
        fresh_scores = jnp.dot(query_rows, new_rot[:, request, head_id].T, preferred_element_type=jnp.float32) * score_scale
        fresh_mask = step_ids <= step_id
        row_top, weights, fresh_weights = softmax_terms(scores, valid_mask[None, :], fresh_scores, fresh_mask[None, :])
        denominator = jnp.sum(weights, axis=-1) + jnp.sum(fresh_weights, axis=-1)
        weighted = jnp.dot(weights, value_rows.astype(jnp.float32), precision=lax.Precision.HIGHEST)
        weighted = weighted + jnp.dot(fresh_weights, new_values[:, request, head_id].astype(jnp.float32), precision=lax.Precision.HIGHEST)
        return weighted / denominator[:, None]

    results = lax.map(one_list, jnp.arange(STEPS * REQS * KVH, dtype=jnp.int32))
    attn = results.reshape(STEPS * REQS, H * HD).astype(jnp.bfloat16)
    projected = jnp.dot(attn, out_weight, preferred_element_type=jnp.float32)
    return projected.reshape(STEPS, REQS, -1).astype(jnp.bfloat16)
```

```python
import functools
import math

import jax
import jax.numpy as jnp
import numpy as np
from jax import lax
from jax.experimental import pallas as pl
from jax.experimental.pallas import tpu as pltpu
from jax.sharding import PartitionSpec as P

BLOCK = 8
ROPE_THETA = 500000.0
NEG_FLOOR = -1e30
MESH = pl.DeviceIdType.MESH


def rope_freqs(head_dim):
    exponent = np.arange(head_dim // 2, dtype=np.float64) * (2.0 / head_dim)
    base = np.power(ROPE_THETA, -exponent)
    wavelength = 2.0 * math.pi / base
    smooth = (8192.0 / wavelength - 1.0) / 3.0
    middle = (1.0 - smooth) * base / 8.0 + smooth * base
    freqs = np.where(wavelength < 2048.0, base, np.where(wavelength > 8192.0, base / 8.0, middle))
    return freqs.astype(np.float32).astype(np.float64)


def rope_tables(positions, head_dim):
    angles = positions[:, None].astype(np.float64) * rope_freqs(head_dim)[None, :]
    cosine, sine = np.cos(angles), np.sin(angles)
    return (
        np.concatenate([cosine, cosine], -1).astype(np.float32),
        np.concatenate([sine, sine], -1).astype(np.float32),
    )


def rotate(x, cosine, signed_sine):
    half = x.shape[-1] // 2
    swapped = jnp.concatenate([x[..., half:], x[..., :half]], axis=-1)
    return x * cosine + swapped * signed_sine


def attend_kernel(
    steps, head_dim, me_ref, base_ref, cos_ref, sin_ref, expand_ref, q_ref, nk_ref, nv_ref,
    mask_ref, factor_ref, basis_ref, value_ref, out_ref, stat_ref, cos_s, sin_s,
):
    r = pl.program_id(0)
    tokens = factor_ref.shape[1]
    pairs = q_ref.shape[1]
    rows = q_ref.shape[2]
    half = rows // 2
    part = half // 2
    wide = 2 * head_dim
    scale = head_dim ** -0.5
    lanes = stat_ref.shape[3]

    @pl.when(r == 0)
    def _():
        sign = jnp.where(
            lax.broadcasted_iota(jnp.int32, (tokens, head_dim), 1) < head_dim // 2, -1.0, 1.0
        )
        base_cos, base_sin = base_ref[0:1], base_ref[1:2]
        c, s = cos_ref[...], sin_ref[...]
        cos_s[...] = base_cos * c - base_sin * s
        sin_s[...] = (base_sin * c + base_cos * s) * sign
        stat_ref[...] = jnp.zeros_like(stat_ref)

    cosine, sine = cos_s[...], sin_s[...]
    holds_new = me_ref[0] == 0
    step_of = lax.broadcasted_iota(jnp.int32, (rows, steps), 0) % steps
    fresh_ok = (lax.broadcasted_iota(jnp.int32, (rows, steps), 1) <= step_of) & holds_new
    spot = lax.broadcasted_iota(jnp.int32, (part, lanes), 1) == (
        lax.broadcasted_iota(jnp.int32, (part, lanes), 0) + r * part
    )
    factors = factor_ref[0]
    for p in range(pairs):
        cols = slice(p * wide, (p + 1) * wide)
        keys = jnp.dot(factors, basis_ref[0, :, cols], preferred_element_type=jnp.float32)
        turned = []
        for u in range(2):
            k = keys[:, u * head_dim : (u + 1) * head_dim]
            turned.append(
                (k * cosine + pltpu.roll(k, head_dim // 2, 1) * sine).astype(jnp.bfloat16)
            )
        keys = jnp.concatenate(turned, axis=1)
        q = q_ref[0, p]
        zero = jnp.zeros((half, head_dim), q.dtype)
        q = jnp.concatenate(
            [jnp.concatenate([q[:half], zero], 1), jnp.concatenate([zero, q[half:]], 1)], 0
        )
        contract = (((1,), (1,)), ((), ()))
        scores = lax.dot_general(q, keys, contract, preferred_element_type=jnp.float32) * scale
        bias = jnp.dot(mask_ref[0, p], expand_ref[...], preferred_element_type=jnp.float32)
        scores = (
            scores.reshape(2, half // steps, steps, tokens) + bias.reshape(2, 1, steps, tokens)
        ).reshape(rows, tokens)
        fresh = (
            lax.dot_general(q, nk_ref[0, :, cols], contract, preferred_element_type=jnp.float32)
            * scale
        )
        fresh = jnp.where(fresh_ok, fresh, NEG_FLOOR)
        top = jnp.maximum(
            jnp.max(scores, axis=1, keepdims=True), jnp.max(fresh, axis=1, keepdims=True)
        )
        weights = jnp.exp(scores - top).astype(jnp.bfloat16)
        fresh_weights = jnp.exp(fresh - top).astype(jnp.bfloat16)
        total = jnp.sum(weights.astype(jnp.float32), axis=1, keepdims=True) + jnp.sum(
            fresh_weights.astype(jnp.float32), axis=1, keepdims=True
        )
        out = jnp.dot(weights, value_ref[0, :, cols], preferred_element_type=jnp.float32)
        out = out + jnp.dot(fresh_weights, nv_ref[0, :, cols], preferred_element_type=jnp.float32)
        for u in range(2):
            for c in range(2):
                at = u * half + c * part
                out_ref[c, 2 * p + u, 0] = out[
                    at : at + part, u * head_dim : (u + 1) * head_dim
                ].astype(out_ref.dtype)
                for i, column in enumerate((top, total)):
                    stat_ref[c, 2 * p + u, i : i + 1] += jnp.sum(
                        jnp.where(spot, column[at : at + part], 0.0), axis=0, keepdims=True
                    )


def combine_kernel(
    chips, reqs, steps, o_ref, st_ref, w_ref, out_ref, w_s, o1, st1, o2s, st2s, o2r, st2r,
    t1s, t1r, t2s, t2r, w_sem, s_o1, r_o1, s_st1, r_st1, s_o2, r_o2, s_st2, r_st2,
    s_t1, r_t1, s_t2, r_t2,
):
    me = lax.axis_index("store")
    chip, core = me // 2, me % 2
    twin = chip * 2 + 1 - core
    rows = o_ref.shape[2]
    head_dim = o_ref.shape[3]
    heads = rows // (reqs * steps)
    width = out_ref.shape[1]

    weight_copy = pltpu.make_async_copy(w_ref, w_s, w_sem)
    weight_copy.start()

    def chip_at(i):
        return lax.rem(chip + i, chips)

    def remote(src, dst, send, recv, device):
        return pltpu.make_async_remote_copy(
            src_ref=src, dst_ref=dst, send_sem=send, recv_sem=recv,
            device_id={"store": device}, device_id_type=MESH,
        )

    barrier = pltpu.get_barrier_semaphore()
    pl.semaphore_signal(barrier, inc=1, device_id={"store": twin}, device_id_type=MESH)

    def greet(i, carry):
        pl.semaphore_signal(
            barrier, inc=1, device_id={"store": chip_at(i) * 2 + core}, device_id_type=MESH
        )
        return carry

    lax.fori_loop(1, chips, greet, 0)
    pl.semaphore_wait(barrier, chips)

    def first(k):
        return (
            remote(o_ref.at[1 - core, k], o1.at[k], s_o1.at[k], r_o1.at[k], twin),
            remote(st_ref.at[1 - core, k], st1.at[k], s_st1.at[k], r_st1.at[k], twin),
        )

    def second(k, slot):
        device = k * 2 + core
        return (
            remote(o2s.at[k], o2r.at[slot], s_o2.at[k], r_o2.at[slot], device),
            remote(st2s.at[k], st2r.at[slot], s_st2.at[k], r_st2.at[slot], device),
        )

    def third(k):
        return remote(t1s.at[k], t1r.at[k], s_t1.at[k], r_t1.at[k], twin)

    def fourth(k, slot):
        return remote(t2s.at[k], t2r.at[slot], s_t2.at[k], r_t2.at[slot], k * 2 + core)

    def send_first(i, carry):
        for copy in first(chip_at(i)):
            copy.start()
        return carry

    lax.fori_loop(1, chips + 1, send_first, 0)

    def merged(k):
        for copy in first(k):
            copy.wait_recv()
        a, b = st_ref[core, k], st1[k]
        top = jnp.maximum(a[0:1], b[0:1])
        scale_a, scale_b = jnp.exp(a[0:1] - top), jnp.exp(b[0:1] - top)
        total = scale_a * a[1:2] + scale_b * b[1:2]
        pad = jnp.zeros((6, rows), jnp.float32)
        columns = jnp.concatenate([scale_a, scale_b, pad], 0).T
        mixed = (
            o_ref[core, k].astype(jnp.float32) * columns[:, 0:1]
            + o1[k].astype(jnp.float32) * columns[:, 1:2]
        )
        return mixed.astype(jnp.bfloat16), jnp.concatenate([top, total, pad], 0)

    def send_second(i, carry):
        k = chip_at(i)
        o2s[k], st2s[k] = merged(k)
        for copy in second(k, chip):
            copy.start()
        return carry

    lax.fori_loop(1, chips, send_second, 0)
    o2r[chip], st2r[chip] = merged(chip)

    def wait_second(i, carry):
        k = chip_at(i)
        for copy in second(k, k):
            copy.wait_recv()
        return carry

    lax.fori_loop(1, chips, wait_second, 0)
    tops = st2r[:, 0, :]
    share = jnp.exp(tops - jnp.max(tops, axis=0, keepdims=True))
    share = share / jnp.sum(share * st2r[:, 1, :], axis=0, keepdims=True)
    columns = share.T
    attn = o2r[0].astype(jnp.float32) * columns[:, 0:1]
    for k in range(1, chips):
        attn = attn + o2r[k].astype(jnp.float32) * columns[:, k : k + 1]
    flat = jnp.concatenate(
        [
            jnp.concatenate(
                [
                    attn[(r * heads + j) * steps : (r * heads + j + 1) * steps]
                    for r in range(reqs)
                ],
                0,
            )
            for j in range(heads)
        ],
        1,
    ).astype(jnp.bfloat16)
    weight_copy.wait()

    def term(k, which):
        at = pl.multiple_of((2 * k + which) * width, width)
        return jnp.dot(flat, w_s[:, pl.ds(at, width)], preferred_element_type=jnp.float32)

    def send_third(i, carry):
        k = chip_at(i)
        t1s[k] = term(k, 1 - core).astype(jnp.bfloat16)
        third(k).start()
        return carry

    lax.fori_loop(1, chips + 1, send_third, 0)

    def summed(k):
        mine = term(k, core)
        third(k).wait_recv()
        return mine + t1r[k].astype(jnp.float32)

    def send_fourth(i, carry):
        k = chip_at(i)
        t2s[k] = summed(k).astype(jnp.bfloat16)
        fourth(k, chip).start()
        return carry

    lax.fori_loop(1, chips, send_fourth, 0)
    own = summed(chip)

    def add_fourth(i, total):
        k = chip_at(i)
        fourth(k, k).wait_recv()
        return total + t2r[k].astype(jnp.float32)

    out_ref[...] = lax.fori_loop(1, chips, add_fourth, own).astype(out_ref.dtype)

    def drain(i, carry):
        k = chip_at(i)
        for copy in first(k) + second(k, k) + (third(k), fourth(k, k)):
            copy.wait_send()
        return carry

    lax.fori_loop(1, chips, drain, 0)
    for copy in first(chip) + (third(chip),):
        copy.wait_send()


def per_device(
    queries, new_keys, new_values, key_factors, key_basis, values, block_index, block_count,
    out_weight,
):
    devices = lax.axis_size("store")
    me = lax.axis_index("store")
    chips = devices // 2
    steps, reqs, n_heads, head_dim = queries.shape
    groups = new_keys.shape[2]
    group = n_heads // groups
    tokens = values.shape[1]
    rank = key_factors.shape[2]
    blocks = tokens // BLOCK
    heads_dev = n_heads // devices
    slots = block_index.shape[-1]
    pairs = groups // 2
    half_group = group // 2
    rows = 2 * group * steps
    part = half_group * steps
    wide = groups * head_dim
    chips_group = half_group // heads_dev

    cos_off, sin_off = rope_tables(np.arange(tokens), head_dim)
    base_tab = np.stack(rope_tables(np.arange(devices) * tokens, head_dim), 1)
    base = lax.dynamic_index_in_dim(jnp.asarray(base_tab), me, 0, keepdims=False)
    sign = np.where(np.arange(head_dim) < head_dim // 2, -1.0, 1.0).astype(np.float32)
    cos_new, sin_new = rope_tables(tokens * devices + np.arange(steps), head_dim)
    cos_new, sin_new = cos_new[:, None, None], (sin_new * sign)[:, None, None]
    q_rot = rotate(queries.astype(jnp.float32), cos_new, sin_new).astype(jnp.bfloat16)
    new_rot = rotate(new_keys.astype(jnp.float32), cos_new, sin_new).astype(jnp.bfloat16)
    q_rot = q_rot.reshape(steps, reqs, groups, chips_group, 2, heads_dev, head_dim)
    q_rot = q_rot.transpose(1, 2, 4, 3, 5, 0, 6).reshape(reqs, pairs, rows, head_dim)
    new_rot = new_rot.transpose(1, 0, 2, 3).reshape(reqs, steps, wide)
    new_val = new_values.transpose(1, 0, 2, 3).reshape(reqs, steps, wide)
    local = block_index - me * blocks
    local = jnp.where(jnp.arange(slots, dtype=jnp.int32) < block_count[..., None], local, -1)
    chosen = jnp.any(local[..., None, :] == jnp.arange(blocks, dtype=jnp.int32)[:, None], axis=-1)
    mask = jnp.where(chosen, 0.0, NEG_FLOOR).astype(jnp.bfloat16)
    mask = mask.transpose(1, 2, 0, 3).reshape(reqs, pairs, 2 * steps, blocks)
    expand = (np.arange(tokens)[None, :] // BLOCK == np.arange(blocks)[:, None]).astype(
        jnp.bfloat16
    )

    def whole(shape):
        return pl.BlockSpec(shape, lambda r: (0,) * len(shape))

    def per_request(shape):
        return pl.BlockSpec((1,) + shape, lambda r: (r,) + (0,) * len(shape))

    lanes = reqs * part
    partial, stats = pl.pallas_call(
        functools.partial(attend_kernel, steps, head_dim),
        grid=(reqs,),
        out_shape=(
            jax.ShapeDtypeStruct((2, groups, reqs, part, head_dim), jnp.bfloat16),
            jax.ShapeDtypeStruct((2, groups, 8, lanes), jnp.float32),
        ),
        in_specs=[
            pl.BlockSpec(memory_space=pltpu.SMEM),
            whole((2, head_dim)),
            whole((tokens, head_dim)),
            whole((tokens, head_dim)),
            whole((blocks, tokens)),
            per_request((pairs, rows, head_dim)),
            per_request((steps, wide)),
            per_request((steps, wide)),
            per_request((pairs, 2 * steps, blocks)),
            per_request((tokens, rank)),
            per_request((rank, wide)),
            per_request((tokens, wide)),
        ],
        out_specs=(
            pl.BlockSpec((2, groups, 1, part, head_dim), lambda r: (0, 0, r, 0, 0)),
            whole((2, groups, 8, lanes)),
        ),
        scratch_shapes=[pltpu.VMEM((tokens, head_dim), jnp.float32)] * 2,
        compiler_params=pltpu.CompilerParams(vmem_limit_bytes=40 * 2**20),
        name="attend",
    )(
        me.reshape(1).astype(jnp.int32), base, cos_off, sin_off, expand, q_rot, new_rot, new_val,
        mask, key_factors, key_basis, values,
    )
    rows_dev = reqs * heads_dev * steps
    partial = partial.reshape(2, groups, reqs, chips_group, heads_dev * steps, head_dim)
    partial = partial.transpose(0, 1, 3, 2, 4, 5).reshape(2, chips, rows_dev, head_dim)
    stats = stats.reshape(2, groups, 8, reqs, chips_group, heads_dev * steps)
    stats = stats.transpose(0, 1, 4, 2, 3, 5).reshape(2, chips, 8, rows_dev)

    width = out_weight.shape[1] // devices
    out_rows = reqs * steps
    dma = pltpu.SemaphoreType.DMA
    vmem = pl.BlockSpec(memory_space=pltpu.VMEM)
    out = pl.pallas_call(
        functools.partial(combine_kernel, chips, reqs, steps),
        out_shape=jax.ShapeDtypeStruct((out_rows, width), jnp.bfloat16),
        in_specs=[vmem, vmem, pl.BlockSpec(memory_space=pl.ANY)],
        out_specs=vmem,
        scratch_shapes=[pltpu.VMEM(out_weight.shape, out_weight.dtype)]
        + [
            pltpu.VMEM((chips, rows_dev, head_dim), jnp.bfloat16),
            pltpu.VMEM((chips, 8, rows_dev), jnp.float32),
        ]
        * 3
        + [pltpu.VMEM((chips, out_rows, width), jnp.bfloat16)] * 4
        + [dma]
        + [dma((chips,))] * 12,
        compiler_params=pltpu.CompilerParams(
            collective_id=0, has_side_effects=True, vmem_limit_bytes=40 * 2**20
        ),
        name="combine",
    )(partial, stats, out_weight)
    return out.reshape(reqs, steps, width).transpose(1, 0, 2)


def solution(mesh):
    placed = (
        P(None, "parts", None, None),
        P(None, "parts", None, None),
        P(None, "parts", None, None),
        P("parts", "store", None),
        P("parts", None, None),
        P("parts", "store", None),
        P(None, "parts", None, None),
        P(None, "parts", None),
        P("store", None),
    )
    return jax.shard_map(
        per_device, mesh=mesh, in_specs=placed, out_specs=P(None, "parts", "store"), check_vma=False
    )
```

```python
import functools
import math

import jax
import jax.numpy as jnp
import numpy as np
from jax import lax
from jax.experimental import pallas as pl
from jax.experimental.pallas import tpu as pltpu
from jax.sharding import PartitionSpec as P

BLOCK = 8
ROPE_THETA = 500000.0
NEG_FLOOR = -1e30
MESH = pl.DeviceIdType.MESH


def rope_freqs(head_dim):
    exponent = np.arange(head_dim // 2, dtype=np.float64) * (2.0 / head_dim)
    base = np.power(ROPE_THETA, -exponent)
    wavelength = 2.0 * math.pi / base
    smooth = (8192.0 / wavelength - 1.0) / 3.0
    middle = (1.0 - smooth) * base / 8.0 + smooth * base
    freqs = np.where(wavelength < 2048.0, base, np.where(wavelength > 8192.0, base / 8.0, middle))
    return freqs.astype(np.float32).astype(np.float64)


def rope_tables(positions, head_dim):
    angles = positions[:, None].astype(np.float64) * rope_freqs(head_dim)[None, :]
    cosine, sine = np.cos(angles), np.sin(angles)
    return (
        np.concatenate([cosine, cosine], -1).astype(np.float32),
        np.concatenate([sine, sine], -1).astype(np.float32),
    )


def attend_kernel(
    steps, head_dim, base_ref, cos_ref, sin_ref, new_cos_ref, new_sin_ref, expand_ref, x_ref,
    list_ref, factor_ref, basis_ref, value_ref, send_ref, keep_ref, stat_ref, cos_s, sin_s,
):
    r = pl.program_id(0)
    me = lax.axis_index("store")
    core = me % 2
    tokens = value_ref.shape[1]
    groups = value_ref.shape[2] // head_dim
    n_heads = x_ref.shape[1] - 2 * groups
    group = n_heads // groups
    blocks = expand_ref.shape[0]
    slots = list_ref.shape[2]
    half = group * steps
    part = half // 2
    rows = 2 * half
    wide = 2 * head_dim
    turn = head_dim // 2
    scale = head_dim ** -0.5
    lanes = stat_ref.shape[3]

    @pl.when(r == 0)
    def _():
        sign = jnp.where(
            lax.broadcasted_iota(jnp.int32, (tokens, head_dim), 1) < turn, -1.0, 1.0
        )
        base = base_ref[me]
        base_cos, base_sin = base[0:1], base[1:2]
        c, s = cos_ref[...], sin_ref[...]
        cos_s[...] = base_cos * c - base_sin * s
        sin_s[...] = (base_sin * c + base_cos * s) * sign
        stat_ref[...] = jnp.zeros_like(stat_ref)

    listed = list_ref[0].astype(jnp.float32).T
    block_ids = (
        lax.broadcasted_iota(jnp.int32, (blocks, groups * steps), 0) + me * blocks
    ).astype(jnp.float32)
    mask = jnp.full((blocks, groups * steps), NEG_FLOOR, jnp.float32)
    for j in range(slots):
        mask = jnp.where(listed[j : j + 1] == block_ids, 0.0, mask)
    bias_all = lax.dot_general(
        mask.astype(jnp.bfloat16), expand_ref[...], (((0,), (0,)), ((), ())),
        preferred_element_type=jnp.float32,
    )

    heads = x_ref[0, : n_heads + groups].astype(jnp.float32)
    heads = heads.reshape((n_heads + groups) * steps, head_dim)
    count = n_heads + groups
    swapped = pltpu.roll(heads, turn, 1).reshape(count, steps, head_dim)
    turned = heads.reshape(count, steps, head_dim) * new_cos_ref[...] + swapped * new_sin_ref[...]
    q_all = turned[:n_heads].reshape(n_heads * steps, head_dim).astype(jnp.bfloat16)
    nk_all = turned[n_heads:]
    nv_all = x_ref[0, n_heads + groups :].astype(jnp.float32)

    cosine, sine = cos_s[...], sin_s[...]
    step_of = lax.broadcasted_iota(jnp.int32, (rows, steps), 0) % steps
    fresh_ok = (lax.broadcasted_iota(jnp.int32, (rows, steps), 1) <= step_of) & (me == 0)
    spot = lax.broadcasted_iota(jnp.int32, (part, lanes), 1) == (
        lax.broadcasted_iota(jnp.int32, (part, lanes), 0) + r * part
    )
    contract = (((1,), (1,)), ((), ()))
    zero = jnp.zeros((half, head_dim), jnp.bfloat16)
    for p in range(groups // 2):
        cols = slice(p * wide, (p + 1) * wide)
        keys = lax.dot_general(
            factor_ref[0], basis_ref[0, :, cols], (((0,), (0,)), ((), ())),
            preferred_element_type=jnp.float32,
        )
        keys = jnp.concatenate(
            [
                (k * cosine + pltpu.roll(k, turn, 1) * sine).astype(jnp.bfloat16)
                for k in (keys[:, :head_dim], keys[:, head_dim:])
            ],
            axis=1,
        )
        q = q_all[p * rows : (p + 1) * rows]
        q = jnp.concatenate(
            [jnp.concatenate([q[:half], zero], 1), jnp.concatenate([zero, q[half:]], 1)], 0
        )
        nk = jnp.concatenate([nk_all[2 * p], nk_all[2 * p + 1]], 1).astype(jnp.bfloat16)
        nv = jnp.concatenate([nv_all[2 * p], nv_all[2 * p + 1]], 1).astype(jnp.bfloat16)
        scores = lax.dot_general(q, keys, contract, preferred_element_type=jnp.float32) * scale
        bias = bias_all[p * 2 * steps : (p + 1) * 2 * steps]
        scores = (
            scores.reshape(2, group, steps, tokens) + bias.reshape(2, 1, steps, tokens)
        ).reshape(rows, tokens)
        fresh = lax.dot_general(q, nk, contract, preferred_element_type=jnp.float32) * scale
        fresh = jnp.where(fresh_ok, fresh, NEG_FLOOR)
        top = jnp.maximum(
            jnp.max(scores, axis=1, keepdims=True), jnp.max(fresh, axis=1, keepdims=True)
        )
        weights = jnp.exp(scores - top)
        fresh = jnp.exp(fresh - top)
        total = jnp.sum(weights, axis=1, keepdims=True) + jnp.sum(fresh, axis=1, keepdims=True)

        def split_dot(w, v):
            high = w.astype(jnp.bfloat16)
            low = (w - high.astype(jnp.float32)).astype(jnp.bfloat16)
            both = jnp.dot(
                jnp.concatenate([high, low], 0), v, preferred_element_type=jnp.float32
            )
            return both[:rows] + both[rows:]

        out = split_dot(weights, value_ref[0, :, cols]) + split_dot(fresh, nv)
        for u in range(2):
            g = 2 * p + u
            mine = out[u * half : (u + 1) * half, u * head_dim : (u + 1) * head_dim]
            keep_ref[g, 0] = jnp.where(core == 0, mine[:part], mine[part:])
            send_ref[g, 0] = jnp.where(core == 0, mine[part:], mine[:part]).astype(jnp.bfloat16)
            for c in range(2):
                at = u * half + c * part
                for i, column in enumerate((top, total)):
                    stat_ref[c, i, g : g + 1] += jnp.sum(
                        jnp.where(spot, column[at : at + part], 0.0), axis=0, keepdims=True
                    )


def combine_kernel(
    chips, reqs, steps, send_ref, keep_ref, st_ref, w_ref, out_ref, w_s, o1, sts, own_w, twin_w,
    o2s, o2r, t1s, t1r, t2s, t2r, w_sem, s_o1, r_o1, s_st, r_st, s_o2, r_o2, s_t1, r_t1, s_t2,
    r_t2,
):
    me = lax.axis_index("store")
    chip, core = me // 2, me % 2
    twin = chip * 2 + 1 - core
    devices = 2 * chips
    rows = send_ref.shape[1]
    head_dim = send_ref.shape[2]
    heads = rows // (reqs * steps)
    width = out_ref.shape[1]

    weight_copy = pltpu.make_async_copy(w_ref, w_s, w_sem)
    weight_copy.start()

    def chip_at(i):
        return lax.rem(chip + i, chips)

    def device_at(i):
        return lax.rem(me + i, devices)

    def remote(src, dst, send, recv, device):
        return pltpu.make_async_remote_copy(
            src_ref=src, dst_ref=dst, send_sem=send, recv_sem=recv,
            device_id={"store": device}, device_id_type=MESH,
        )

    barrier = pltpu.get_barrier_semaphore()

    def greet(i, carry):
        pl.semaphore_signal(
            barrier, inc=1, device_id={"store": device_at(i)}, device_id_type=MESH
        )
        return carry

    lax.fori_loop(1, devices, greet, 0)
    pl.semaphore_wait(barrier, devices - 1)

    first = remote(send_ref, o1, s_o1, r_o1, twin)

    def gather(d, slot):
        return remote(st_ref.at[lax.rem(d, 2)], sts.at[slot], s_st.at[d], r_st.at[slot], d)

    def second(k, slot):
        return remote(o2s.at[k], o2r.at[slot], s_o2.at[k], r_o2.at[slot], k * 2 + core)

    def third(k):
        return remote(t1s.at[k], t1r.at[k], s_t1.at[k], r_t1.at[k], twin)

    def fourth(k, slot):
        return remote(t2s.at[k], t2r.at[slot], s_t2.at[k], r_t2.at[slot], k * 2 + core)

    def send_stats(i, carry):
        gather(device_at(i), me).start()
        return carry

    lax.fori_loop(1, devices, send_stats, 0)
    first.start()
    sts[me] = st_ref[core]

    def wait_stats(i, carry):
        d = device_at(i)
        gather(d, d).wait_recv()
        return carry

    lax.fori_loop(1, devices, wait_stats, 0)
    top = sts[0, 0]
    for d in range(1, devices):
        top = jnp.maximum(top, sts[d, 0])
    total = jnp.exp(sts[0, 0] - top) * sts[0, 1]
    for d in range(1, devices):
        total = total + jnp.exp(sts[d, 0] - top) * sts[d, 1]
    columns = jnp.concatenate(
        [jnp.exp(sts[me, 0] - top) / total, jnp.exp(sts[twin, 0] - top) / total], 0
    ).T
    for k in range(chips):
        own_w[k] = jnp.broadcast_to(columns[:, k : k + 1], (rows, head_dim))
        twin_w[k] = jnp.broadcast_to(columns[:, chips + k : chips + k + 1], (rows, head_dim))
    first.wait_recv()

    def merged(k):
        return keep_ref[k] * own_w[k] + o1[k].astype(jnp.float32) * twin_w[k]

    def send_second(i, carry):
        k = chip_at(i)
        o2s[k] = merged(k).astype(jnp.bfloat16)
        second(k, chip).start()
        return carry

    lax.fori_loop(1, chips, send_second, 0)

    def add_second(i, attn):
        k = chip_at(i)
        second(k, k).wait_recv()
        return attn + o2r[k].astype(jnp.float32)

    attn = lax.fori_loop(1, chips, add_second, merged(chip))
    flat = jnp.concatenate(
        [
            jnp.concatenate(
                [
                    attn[(r * heads + j) * steps : (r * heads + j + 1) * steps]
                    for r in range(reqs)
                ],
                0,
            )
            for j in range(heads)
        ],
        1,
    ).astype(jnp.bfloat16)
    weight_copy.wait()

    def term(k, which):
        at = pl.multiple_of((2 * k + which) * width, width)
        return jnp.dot(flat, w_s[:, pl.ds(at, width)], preferred_element_type=jnp.float32)

    def send_third(i, carry):
        k = chip_at(i)
        t1s[k] = term(k, 1 - core).astype(jnp.bfloat16)
        third(k).start()
        return carry

    lax.fori_loop(1, chips + 1, send_third, 0)

    def summed(k):
        mine = term(k, core)
        third(k).wait_recv()
        return mine + t1r[k].astype(jnp.float32)

    def send_fourth(i, carry):
        k = chip_at(i)
        t2s[k] = summed(k).astype(jnp.bfloat16)
        fourth(k, chip).start()
        return carry

    lax.fori_loop(1, chips, send_fourth, 0)
    own = summed(chip)

    def add_fourth(i, total):
        k = chip_at(i)
        fourth(k, k).wait_recv()
        return total + t2r[k].astype(jnp.float32)

    out_ref[...] = lax.fori_loop(1, chips, add_fourth, own).astype(out_ref.dtype)

    def drain(i, carry):
        k = chip_at(i)
        for copy in (second(k, k), third(k), fourth(k, k)):
            copy.wait_send()
        return carry

    def drain_stats(i, carry):
        gather(device_at(i), me).wait_send()
        return carry

    lax.fori_loop(1, chips, drain, 0)
    lax.fori_loop(1, devices, drain_stats, 0)
    first.wait_send()
    third(chip).wait_send()


def per_device(
    queries, new_keys, new_values, key_factors, key_basis, values, block_index, block_count,
    out_weight,
):
    devices = lax.axis_size("store")
    chips = devices // 2
    steps, reqs, n_heads, head_dim = queries.shape
    groups = new_keys.shape[2]
    group = n_heads // groups
    tokens = values.shape[1]
    rank = key_factors.shape[2]
    blocks = tokens // BLOCK
    heads_dev = n_heads // devices
    slots = block_index.shape[-1]
    half_group = group // 2
    part = half_group * steps
    wide = groups * head_dim
    chips_group = half_group // heads_dev

    cos_off, sin_off = rope_tables(np.arange(tokens), head_dim)
    base = np.stack(rope_tables(np.arange(devices) * tokens, head_dim), 1)
    sign = np.where(np.arange(head_dim) < head_dim // 2, -1.0, 1.0).astype(np.float32)
    cos_new, sin_new = rope_tables(tokens * devices + np.arange(steps), head_dim)
    q = queries
    if chips_group > 1:
        q = q.reshape(steps, reqs, groups, chips_group, 2, heads_dev, head_dim)
        q = q.swapaxes(3, 4).reshape(queries.shape)
    x = jnp.concatenate([q, new_keys, new_values], axis=2).transpose(1, 2, 0, 3)
    lists = jnp.where(
        jnp.arange(slots, dtype=jnp.int32) < block_count[..., None], block_index, -1
    )
    lists = lists.transpose(1, 2, 0, 3).reshape(reqs, groups * steps, slots)
    expand = (np.arange(tokens)[None, :] // BLOCK == np.arange(blocks)[:, None]).astype(
        jnp.bfloat16
    )

    def whole(shape):
        return pl.BlockSpec(shape, lambda r: (0,) * len(shape))

    def per_request(shape):
        return pl.BlockSpec((1,) + shape, lambda r: (r,) + (0,) * len(shape))

    lanes = reqs * part
    out_block = pl.BlockSpec((groups, 1, part, head_dim), lambda r: (0, r, 0, 0))
    send, keep, stats = pl.pallas_call(
        functools.partial(attend_kernel, steps, head_dim),
        grid=(reqs,),
        out_shape=(
            jax.ShapeDtypeStruct((groups, reqs, part, head_dim), jnp.bfloat16),
            jax.ShapeDtypeStruct((groups, reqs, part, head_dim), jnp.float32),
            jax.ShapeDtypeStruct((2, 2, groups, lanes), jnp.float32),
        ),
        in_specs=[
            whole((devices, 2, head_dim)),
            whole((tokens, head_dim)),
            whole((tokens, head_dim)),
            whole((steps, head_dim)),
            whole((steps, head_dim)),
            whole((blocks, tokens)),
            per_request((n_heads + 2 * groups, steps, head_dim)),
            per_request((groups * steps, slots)),
            per_request((rank, tokens)),
            per_request((rank, wide)),
            per_request((tokens, wide)),
        ],
        out_specs=(out_block, out_block, whole((2, 2, groups, lanes))),
        scratch_shapes=[pltpu.VMEM((tokens, head_dim), jnp.float32)] * 2,
        compiler_params=pltpu.CompilerParams(vmem_limit_bytes=60 * 2**20),
        name="attend",
    )(
        base, cos_off, sin_off, cos_new, sin_new * sign, expand, x, lists,
        key_factors.swapaxes(1, 2), key_basis, values,
    )
    rows_dev = reqs * heads_dev * steps

    def by_chip(y):
        y = y.reshape(groups, reqs, chips_group, heads_dev * steps, head_dim)
        return y.transpose(0, 2, 1, 3, 4).reshape(chips, rows_dev, head_dim)

    stats = stats.reshape(2, 2, groups, reqs, chips_group, heads_dev * steps)
    stats = stats.transpose(0, 1, 2, 4, 3, 5).reshape(2, 2, chips, rows_dev)

    width = out_weight.shape[1] // devices
    out_rows = reqs * steps
    dma = pltpu.SemaphoreType.DMA
    vmem = pl.BlockSpec(memory_space=pltpu.VMEM)
    out = pl.pallas_call(
        functools.partial(combine_kernel, chips, reqs, steps),
        out_shape=jax.ShapeDtypeStruct((out_rows, width), jnp.bfloat16),
        in_specs=[vmem, vmem, vmem, pl.BlockSpec(memory_space=pl.ANY)],
        out_specs=vmem,
        scratch_shapes=[
            pltpu.VMEM(out_weight.shape, out_weight.dtype),
            pltpu.VMEM((chips, rows_dev, head_dim), jnp.bfloat16),
            pltpu.VMEM((devices, 2, chips, rows_dev), jnp.float32),
            pltpu.VMEM((chips, rows_dev, head_dim), jnp.float32),
            pltpu.VMEM((chips, rows_dev, head_dim), jnp.float32),
            pltpu.VMEM((chips, rows_dev, head_dim), jnp.bfloat16),
            pltpu.VMEM((chips, rows_dev, head_dim), jnp.bfloat16),
        ]
        + [pltpu.VMEM((chips, out_rows, width), jnp.bfloat16)] * 4
        + [dma, dma, dma, dma((devices,)), dma((devices,))]
        + [dma((chips,))] * 6,
        compiler_params=pltpu.CompilerParams(
            collective_id=0, has_side_effects=True, vmem_limit_bytes=60 * 2**20
        ),
        name="combine",
    )(by_chip(send), by_chip(keep), stats, out_weight)
    return out.reshape(reqs, steps, width).transpose(1, 0, 2)


def solution(mesh):
    placed = (
        P(None, "parts", None, None),
        P(None, "parts", None, None),
        P(None, "parts", None, None),
        P("parts", "store", None),
        P("parts", None, None),
        P("parts", "store", None),
        P(None, "parts", None, None),
        P(None, "parts", None),
        P("store", None),
    )
    return jax.shard_map(
        per_device, mesh=mesh, in_specs=placed, out_specs=P(None, "parts", "store"), check_vma=False
    )
```

```python
import functools
import math

import jax
import jax.numpy as jnp
import numpy as np
from jax import lax
from jax.experimental import pallas as pl
from jax.experimental.pallas import tpu as pltpu
from jax.sharding import PartitionSpec as P

BLOCK = 8
ROPE_THETA = 500000.0
NEG_FLOOR = -1e30
MESH = pl.DeviceIdType.MESH


def rope_freqs(head_dim):
    exponent = np.arange(head_dim // 2, dtype=np.float64) * (2.0 / head_dim)
    base = np.power(ROPE_THETA, -exponent)
    wavelength = 2.0 * math.pi / base
    smooth = (8192.0 / wavelength - 1.0) / 3.0
    middle = (1.0 - smooth) * base / 8.0 + smooth * base
    freqs = np.where(wavelength < 2048.0, base, np.where(wavelength > 8192.0, base / 8.0, middle))
    return freqs.astype(np.float32).astype(np.float64)


def rope_tables(positions, head_dim):
    angles = positions[:, None].astype(np.float64) * rope_freqs(head_dim)[None, :]
    cosine, sine = np.cos(angles), np.sin(angles)
    return (
        np.concatenate([cosine, cosine], -1).astype(np.float32),
        np.concatenate([sine, sine], -1).astype(np.float32),
    )


def attend_kernel(
    steps, head_dim, head_order, place, base_ref, cos_ref, sin_ref, new_cos_ref, new_sin_ref,
    expand_ref, q_ref, nk_ref, nv_ref, list_ref, factor_ref, basis_ref, value_ref, send_ref,
    keep_ref, stat_ref, cos_s, sin_s, head_s, nv_s, bias_s,
):
    r = pl.program_id(0)
    me = lax.axis_index("store")
    core = me % 2
    tokens = value_ref.shape[1]
    groups = value_ref.shape[2] // head_dim
    n_heads = q_ref.shape[2]
    group = n_heads // groups
    blocks = expand_ref.shape[0]
    slots = list_ref.shape[3]
    half = group * steps
    part = half // 2
    rows = 2 * half
    wide = 2 * head_dim
    turn = head_dim // 2
    scale = head_dim ** -0.5
    lanes = stat_ref.shape[3]

    @pl.when(r == 0)
    def _():
        sign = jnp.where(
            lax.broadcasted_iota(jnp.int32, (tokens, head_dim), 1) < turn, -1.0, 1.0
        )
        base = base_ref[me]
        base_cos, base_sin = base[0:1], base[1:2]
        c, s = cos_ref[...], sin_ref[...]
        cos_s[...] = base_cos * c - base_sin * s
        sin_s[...] = (base_sin * c + base_cos * s) * sign
        stat_ref[...] = jnp.zeros_like(stat_ref)

    listed = list_ref[:, 0].reshape(steps * groups, slots).astype(jnp.float32).T
    block_ids = (
        lax.broadcasted_iota(jnp.int32, (blocks, groups * steps), 0) + me * blocks
    ).astype(jnp.float32)
    mask = jnp.full((blocks, groups * steps), NEG_FLOOR, jnp.float32)
    for j in range(slots):
        mask = jnp.where(listed[j : j + 1] == block_ids, 0.0, mask)
    bias_all = lax.dot_general(
        mask.astype(jnp.bfloat16), expand_ref[...], (((0,), (0,)), ((), ())),
        preferred_element_type=jnp.float32,
    )
    n_lists = groups * steps
    for c in range(tokens // head_dim):
        bias_s[c * n_lists : (c + 1) * n_lists] = bias_all[:, c * head_dim : (c + 1) * head_dim]

    count = n_heads + groups
    for t in range(steps):
        x = jnp.concatenate(
            [q_ref[t, 0].astype(jnp.float32), nk_ref[t, 0].astype(jnp.float32)], 0
        )
        head_s[t * count : (t + 1) * count] = (
            x * new_cos_ref[t : t + 1] + pltpu.roll(x, turn, 1) * new_sin_ref[t : t + 1]
        )
        nv_s[t * groups : (t + 1) * groups] = nv_ref[t, 0].astype(jnp.float32)

    def of_steps(ref, at, stride):
        return ref[pl.ds(at, steps, stride=stride)]

    cosine, sine = cos_s[...], sin_s[...]
    step_of = lax.broadcasted_iota(jnp.int32, (rows, steps), 0) % steps
    fresh_ok = (lax.broadcasted_iota(jnp.int32, (rows, steps), 1) <= step_of) & (me == 0)
    spot = lax.broadcasted_iota(jnp.int32, (part, lanes), 1) == (
        lax.broadcasted_iota(jnp.int32, (part, lanes), 0) + r * part
    )
    contract = (((1,), (1,)), ((), ()))
    zero = jnp.zeros((half, head_dim), jnp.bfloat16)
    keys_all = lax.dot_general(
        factor_ref[0], basis_ref[0], (((0,), (0,)), ((), ())), preferred_element_type=jnp.float32
    )
    for p in range(groups // 2):
        cols = slice(p * wide, (p + 1) * wide)
        keys = jnp.concatenate(
            [
                (k * cosine + pltpu.roll(k, turn, 1) * sine).astype(jnp.bfloat16)
                for k in (
                    keys_all[:, g * head_dim : (g + 1) * head_dim] for g in (2 * p, 2 * p + 1)
                )
            ],
            axis=1,
        )
        q = jnp.concatenate(
            [of_steps(head_s, h, count) for h in head_order[2 * p * group : 2 * (p + 1) * group]],
            0,
        ).astype(jnp.bfloat16)
        q = jnp.concatenate(
            [jnp.concatenate([q[:half], zero], 1), jnp.concatenate([zero, q[half:]], 1)], 0
        )
        nk = jnp.concatenate(
            [of_steps(head_s, n_heads + 2 * p + u, count) for u in range(2)], 1
        ).astype(jnp.bfloat16)
        nv = jnp.concatenate(
            [of_steps(nv_s, 2 * p + u, groups) for u in range(2)], 1
        ).astype(jnp.bfloat16)
        bias = jnp.concatenate(
            [
                jnp.concatenate(
                    [of_steps(bias_s, c * n_lists + 2 * p + u, groups) for u in range(2)], 0
                )
                for c in range(tokens // head_dim)
            ],
            1,
        )
        scores = lax.dot_general(q, keys, contract, preferred_element_type=jnp.float32) * scale
        scores = (
            scores.reshape(2, group, steps, tokens) + bias.reshape(2, 1, steps, tokens)
        ).reshape(rows, tokens)
        fresh = lax.dot_general(q, nk, contract, preferred_element_type=jnp.float32) * scale
        fresh = jnp.where(fresh_ok, fresh, NEG_FLOOR)
        top = jnp.maximum(
            jnp.max(scores, axis=1, keepdims=True), jnp.max(fresh, axis=1, keepdims=True)
        )
        weights = jnp.exp(scores - top)
        fresh = jnp.exp(fresh - top)
        total = jnp.sum(weights, axis=1, keepdims=True) + jnp.sum(fresh, axis=1, keepdims=True)

        def split_dot(w, v):
            high = w.astype(jnp.bfloat16)
            low = (w - high.astype(jnp.float32)).astype(jnp.bfloat16)
            both = jnp.dot(
                jnp.concatenate([high, low], 0), v, preferred_element_type=jnp.float32
            )
            return both[:rows] + both[rows:]

        out = split_dot(weights, value_ref[0, :, cols]) + split_dot(fresh, nv)
        for u in range(2):
            g = place[2 * p + u]
            mine = out[u * half : (u + 1) * half, u * head_dim : (u + 1) * head_dim]
            keep_ref[g, 0] = jnp.where(core == 0, mine[:part], mine[part:])
            send_ref[g, 0] = jnp.where(core == 0, mine[part:], mine[:part])
            for c in range(2):
                at = u * half + c * part
                for i, column in enumerate((top, total)):
                    stat_ref[c, i, g : g + 1] += jnp.sum(
                        jnp.where(spot, column[at : at + part], 0.0), axis=0, keepdims=True
                    )


def combine_kernel(
    chips, reqs, steps, send_ref, keep_ref, st_ref, w_ref, out_ref, w_s, o1, st1, weight_s, near,
    o2s, o2r, st2s, st2r, o3s, o3r, st3s, st3r, t1s, t1r, t2s, t2r, t3s, t3r, sem, k_sem, z_sem,
):
    me = lax.axis_index("store")
    chip, core = me // 2, me % 2
    lines = chips // 2
    line, side = chip // 2, chip % 2
    twin = chip * 2 + 1 - core
    mate = (line * 2 + 1 - side) * 2 + core
    rows = send_ref.shape[2]
    head_dim = send_ref.shape[3]
    heads = rows // (reqs * steps)
    width = out_ref.shape[1]

    weight_copy = pltpu.make_async_copy(w_ref, w_s, sem.at[0])
    weight_copy.start()

    def line_at(i):
        return lax.rem(line + i, lines)

    def device_of(z):
        return (z * 2 + side) * 2 + core

    def remote(src, dst, send, recv, device):
        return pltpu.make_async_remote_copy(
            src_ref=src, dst_ref=dst, send_sem=send, recv_sem=recv,
            device_id={"store": device}, device_id_type=MESH,
        )

    barrier = pltpu.get_barrier_semaphore()
    for device in (twin, mate):
        pl.semaphore_signal(barrier, inc=1, device_id={"store": device}, device_id_type=MESH)

    def greet(i, carry):
        pl.semaphore_signal(
            barrier, inc=1, device_id={"store": device_of(line_at(i))}, device_id_type=MESH
        )
        return carry

    lax.fori_loop(1, lines, greet, 0)
    pl.semaphore_wait(barrier, lines + 1)

    def loop(start, stop, step):
        def body(i, carry):
            step(line_at(i))
            return carry

        lax.fori_loop(start, stop, body, 0)

    stats_1 = remote(st_ref.at[1 - core], st1, sem.at[1], sem.at[2], twin)
    stats_2 = remote(st2s, st2r, sem.at[3], sem.at[4], mate)

    def first(which):
        return remote(
            send_ref.at[which], o1.at[which], k_sem.at[0, which], k_sem.at[1, which], twin
        )

    def second(z):
        return remote(o2s.at[z], o2r.at[z], z_sem.at[0, z], z_sem.at[1, z], mate)

    def third(z, slot):
        device = device_of(z)
        return (
            remote(st3s.at[z], st3r.at[slot], z_sem.at[2, z], z_sem.at[3, slot], device),
            remote(o3s.at[z], o3r.at[slot], z_sem.at[4, z], z_sem.at[5, slot], device),
        )

    def twin_term(which, z):
        at = which * lines + z
        return remote(t1s.at[at], t1r.at[at], k_sem.at[2, at], k_sem.at[3, at], twin)

    def mate_term(z):
        return remote(t2s.at[z], t2r.at[z], z_sem.at[6, z], z_sem.at[7, z], mate)

    def line_term(z, slot):
        return remote(
            t3s.at[z], t3r.at[slot], z_sem.at[8, z], z_sem.at[9, slot], device_of(z)
        )

    other = 1 - side
    stats_1.start()
    first(other).start()
    first(side).start()

    def join(a_top, a_sum, b_top, b_sum):
        top = jnp.maximum(a_top, b_top)
        a, b = jnp.exp(a_top - top), jnp.exp(b_top - top)
        return top, a * a_sum + b * b_sum, a, b

    def spread(at, columns):
        columns = columns.T
        for k in range(columns.shape[1]):
            weight_s[at + k] = jnp.broadcast_to(columns[:, k : k + 1], (rows, head_dim))

    stats_1.wait_recv()
    my_top, my_sum, a, b = join(st_ref[core, 0], st_ref[core, 1], st1[0], st1[1])

    def side_of(x, which):
        return jnp.where(which == 0, x[:lines], x[lines:])

    st2s[0], st2s[1] = side_of(my_top, other), side_of(my_sum, other)
    stats_2.start()
    spread(0, jnp.concatenate([a, b], 0))

    def joined(which, z):
        k = which * lines + z
        return keep_ref[which, z] * weight_s[k] + o1[which, z] * weight_s[chips + k]

    first(other).wait_recv()

    def send_second(z):
        o2s[z] = joined(other, z).astype(jnp.bfloat16)
        second(z).start()

    loop(1, lines + 1, send_second)
    stats_2.wait_recv()
    near_top, near_sum, a, b = join(
        side_of(my_top, side), side_of(my_sum, side), st2r[0], st2r[1]
    )
    pad = jnp.zeros((6, rows), jnp.float32)
    for z in range(lines):
        st3s[z] = jnp.concatenate([near_top[z : z + 1], near_sum[z : z + 1], pad], 0)
    st3r[line] = st3s[line]
    loop(1, lines, lambda z: third(z, line)[0].start())
    first(side).wait_recv()
    for z in range(lines):
        near[z] = joined(side, z)
    spread(0, jnp.concatenate([a, b], 0))

    def paired(z):
        second(z).wait_recv()
        return near[z] * weight_s[z] + o2r[z].astype(jnp.float32) * weight_s[lines + z]

    def send_third(z):
        o3s[z] = paired(z).astype(jnp.bfloat16)
        third(z, line)[1].start()

    loop(1, lines, send_third)
    own = paired(line)
    loop(1, lines, lambda z: third(z, z)[0].wait_recv())
    tops = st3r[:, 0, :]
    share = jnp.exp(tops - jnp.max(tops, axis=0, keepdims=True))
    share = share / jnp.sum(share * st3r[:, 1, :], axis=0, keepdims=True)
    spread(0, share)

    def add_third(i, attn):
        z = line_at(i)
        third(z, z)[1].wait_recv()
        return attn + o3r[z].astype(jnp.float32) * weight_s[z]

    attn = lax.fori_loop(1, lines, add_third, own * weight_s[line])
    flat = jnp.concatenate(
        [
            jnp.concatenate(
                [
                    attn[(r * heads + j) * steps : (r * heads + j + 1) * steps]
                    for r in range(reqs)
                ],
                0,
            )
            for j in range(heads)
        ],
        1,
    ).astype(jnp.bfloat16)
    weight_copy.wait()

    def term(which, z, half):
        at = pl.multiple_of(((2 * z + which) * 2 + half) * width, width)
        return jnp.dot(flat, w_s[:, pl.ds(at, width)], preferred_element_type=jnp.float32)

    def send_twin(which):
        def step(z):
            t1s[which * lines + z] = term(which, z, 1 - core)
            twin_term(which, z).start()

        loop(1, lines + 1, step)

    def twin_sum(which, z):
        mine = term(which, z, core)
        twin_term(which, z).wait_recv()
        return mine + t1r[which * lines + z]

    def send_mate(z):
        t2s[z] = twin_sum(other, z).astype(jnp.bfloat16)
        mate_term(z).start()

    def mate_sum(z):
        mine = twin_sum(side, z)
        mate_term(z).wait_recv()
        return mine + t2r[z].astype(jnp.float32)

    def send_line(z):
        t3s[z] = mate_sum(z).astype(jnp.bfloat16)
        line_term(z, line).start()

    send_twin(other)
    loop(1, lines + 1, send_mate)
    send_twin(side)
    loop(1, lines, send_line)
    own = mate_sum(line)

    def add_line(i, total):
        z = line_at(i)
        line_term(z, z).wait_recv()
        return total + t3r[z].astype(jnp.float32)

    out_ref[...] = lax.fori_loop(1, lines, add_line, own).astype(out_ref.dtype)

    def drain(z):
        for copy in (second(z), twin_term(0, z), twin_term(1, z), mate_term(z)):
            copy.wait_send()

    def drain_lines(z):
        for copy in third(z, line) + (line_term(z, line),):
            copy.wait_send()

    loop(1, lines + 1, drain)
    loop(1, lines, drain_lines)
    for copy in (stats_1, stats_2, first(0), first(1)):
        copy.wait_send()


def per_device(
    queries, new_keys, new_values, key_factors, key_basis, values, block_index, block_count,
    out_weight,
):
    devices = lax.axis_size("store")
    chips = devices // 2
    steps, reqs, n_heads, head_dim = queries.shape
    groups = new_keys.shape[2]
    group = n_heads // groups
    tokens = values.shape[1]
    rank = key_factors.shape[2]
    blocks = tokens // BLOCK
    heads_dev = n_heads // devices
    slots = block_index.shape[-1]
    half_group = group // 2
    part = half_group * steps
    wide = groups * head_dim
    chips_group = half_group // heads_dev

    cos_off, sin_off = rope_tables(np.arange(tokens), head_dim)
    base = np.stack(rope_tables(np.arange(devices) * tokens, head_dim), 1)
    sign = np.where(np.arange(head_dim) < head_dim // 2, -1.0, 1.0).astype(np.float32)
    cos_new, sin_new = rope_tables(tokens * devices + np.arange(steps), head_dim)
    head_order = np.arange(n_heads).reshape(groups, chips_group, 2, heads_dev)
    head_order = tuple(int(h) for h in head_order.swapaxes(1, 2).reshape(-1))
    lines = chips // 2
    place = [g if chips_group > 1 else (g % 2) * lines + g // 2 for g in range(groups)]
    lists = jnp.where(
        jnp.arange(slots, dtype=jnp.int32) < block_count[..., None], block_index, -1
    )
    expand = (np.arange(tokens)[None, :] // BLOCK == np.arange(blocks)[:, None]).astype(
        jnp.bfloat16
    )

    def whole(shape):
        return pl.BlockSpec(shape, lambda r: (0,) * len(shape))

    def per_request(shape):
        return pl.BlockSpec((1,) + shape, lambda r: (r,) + (0,) * len(shape))

    def of_request(shape):
        return pl.BlockSpec((steps, 1) + shape, lambda r: (0, r) + (0,) * len(shape))

    lanes = reqs * part
    out_block = pl.BlockSpec((groups, 1, part, head_dim), lambda r: (0, r, 0, 0))
    send, keep, stats = pl.pallas_call(
        functools.partial(attend_kernel, steps, head_dim, head_order, place),
        grid=(reqs,),
        out_shape=(
            jax.ShapeDtypeStruct((groups, reqs, part, head_dim), jnp.float32),
            jax.ShapeDtypeStruct((groups, reqs, part, head_dim), jnp.float32),
            jax.ShapeDtypeStruct((2, 2, groups, lanes), jnp.float32),
        ),
        in_specs=[
            whole((devices, 2, head_dim)),
            whole((tokens, head_dim)),
            whole((tokens, head_dim)),
            whole((steps, head_dim)),
            whole((steps, head_dim)),
            whole((blocks, tokens)),
            of_request((n_heads, head_dim)),
            of_request((groups, head_dim)),
            of_request((groups, head_dim)),
            of_request((groups, slots)),
            per_request((rank, tokens)),
            per_request((rank, wide)),
            per_request((tokens, wide)),
        ],
        out_specs=(out_block, out_block, whole((2, 2, groups, lanes))),
        scratch_shapes=[
            pltpu.VMEM((tokens, head_dim), jnp.float32),
            pltpu.VMEM((tokens, head_dim), jnp.float32),
            pltpu.VMEM((steps * (n_heads + groups), head_dim), jnp.float32),
            pltpu.VMEM((steps * groups, head_dim), jnp.float32),
            pltpu.VMEM((steps * groups * tokens // head_dim, head_dim), jnp.float32),
        ],
        compiler_params=pltpu.CompilerParams(vmem_limit_bytes=60 * 2**20),
        name="attend",
    )(
        base, cos_off, sin_off, cos_new, sin_new * sign, expand, queries, new_keys, new_values,
        lists, key_factors.swapaxes(1, 2), key_basis, values,
    )
    rows_dev = reqs * heads_dev * steps

    def by_chip(y):
        if chips_group > 1:
            y = y.reshape(groups, reqs, chips_group, heads_dev * steps, head_dim)
            y = y.transpose(0, 2, 1, 3, 4).reshape(lines, 2, rows_dev, head_dim).swapaxes(0, 1)
        return y.reshape(2, lines, rows_dev, head_dim)

    if chips_group > 1:
        stats = stats.reshape(2, 2, groups, reqs, chips_group, heads_dev * steps)
        stats = stats.transpose(0, 1, 2, 4, 3, 5).reshape(2, 2, lines, 2, rows_dev)
        stats = stats.swapaxes(2, 3).reshape(2, 2, chips, rows_dev)

    width = out_weight.shape[1] // devices
    out_rows = reqs * steps
    dma = pltpu.SemaphoreType.DMA
    vmem = pl.BlockSpec(memory_space=pltpu.VMEM)
    out = pl.pallas_call(
        functools.partial(combine_kernel, chips, reqs, steps),
        out_shape=jax.ShapeDtypeStruct((out_rows, width), jnp.bfloat16),
        in_specs=[vmem, vmem, vmem, pl.BlockSpec(memory_space=pl.ANY)],
        out_specs=vmem,
        scratch_shapes=[
            pltpu.VMEM(out_weight.shape, out_weight.dtype),
            pltpu.VMEM((2, lines, rows_dev, head_dim), jnp.float32),
            pltpu.VMEM((2, chips, rows_dev), jnp.float32),
            pltpu.VMEM((2 * chips, rows_dev, head_dim), jnp.float32),
            pltpu.VMEM((lines, rows_dev, head_dim), jnp.float32),
            pltpu.VMEM((lines, rows_dev, head_dim), jnp.bfloat16),
            pltpu.VMEM((lines, rows_dev, head_dim), jnp.bfloat16),
            pltpu.VMEM((2, lines, rows_dev), jnp.float32),
            pltpu.VMEM((2, lines, rows_dev), jnp.float32),
            pltpu.VMEM((lines, rows_dev, head_dim), jnp.bfloat16),
            pltpu.VMEM((lines, rows_dev, head_dim), jnp.bfloat16),
            pltpu.VMEM((lines, 8, rows_dev), jnp.float32),
            pltpu.VMEM((lines, 8, rows_dev), jnp.float32),
            pltpu.VMEM((chips, out_rows, width), jnp.float32),
            pltpu.VMEM((chips, out_rows, width), jnp.float32),
        ]
        + [pltpu.VMEM((lines, out_rows, width), jnp.bfloat16)] * 4
        + [dma((5,)), dma((4, chips)), dma((10, lines))],
        compiler_params=pltpu.CompilerParams(
            collective_id=0, has_side_effects=True, vmem_limit_bytes=57 * 2**20
        ),
        name="combine",
    )(by_chip(send), by_chip(keep), stats, out_weight)
    return out.reshape(reqs, steps, width).transpose(1, 0, 2)


def solution(mesh):
    placed = (
        P(None, "parts", None, None),
        P(None, "parts", None, None),
        P(None, "parts", None, None),
        P("parts", "store", None),
        P("parts", None, None),
        P("parts", "store", None),
        P(None, "parts", None, None),
        P(None, "parts", None),
        P("store", None),
    )
    return jax.shard_map(
        per_device, mesh=mesh, in_specs=placed, out_specs=P(None, "parts", "store"), check_vma=False
    )
```

```python
import functools
import math

import jax
import jax.numpy as jnp
import numpy as np
from jax import lax
from jax.experimental import pallas as pl
from jax.experimental.pallas import tpu as pltpu
from jax.sharding import PartitionSpec as P

BLOCK = 8
ROPE_THETA = 500000.0
NEG_FLOOR = -1e30
MESH = pl.DeviceIdType.MESH


def rope_freqs(head_dim):
    exponent = np.arange(head_dim // 2, dtype=np.float64) * (2.0 / head_dim)
    base = np.power(ROPE_THETA, -exponent)
    wavelength = 2.0 * math.pi / base
    smooth = (8192.0 / wavelength - 1.0) / 3.0
    middle = (1.0 - smooth) * base / 8.0 + smooth * base
    freqs = np.where(wavelength < 2048.0, base, np.where(wavelength > 8192.0, base / 8.0, middle))
    return freqs.astype(np.float32).astype(np.float64)


def rope_tables(positions, head_dim):
    angles = positions[:, None].astype(np.float64) * rope_freqs(head_dim)[None, :]
    cosine, sine = np.cos(angles), np.sin(angles)
    return (
        np.concatenate([cosine, cosine], -1).astype(np.float32),
        np.concatenate([sine, sine], -1).astype(np.float32),
    )


def attend_kernel(
    steps, head_dim, head_order, place, base_ref, cos_ref, sin_ref, new_cos_ref, new_sin_ref,
    expand_ref, q_ref, nk_ref, nv_ref, list_ref, factor_ref, basis_ref, value_ref, send_ref,
    keep_ref, stat_ref, cos_s, sin_s, head_s, nv_s, bias_s,
):
    r = pl.program_id(0)
    me = lax.axis_index("store")
    core = me % 2
    tokens = value_ref.shape[1]
    groups = value_ref.shape[2] // head_dim
    n_heads = q_ref.shape[2]
    group = n_heads // groups
    blocks = expand_ref.shape[0]
    slots = list_ref.shape[3]
    half = group * steps
    part = half // 2
    rows = 2 * half
    wide = 2 * head_dim
    turn = head_dim // 2
    scale = head_dim ** -0.5
    lanes = stat_ref.shape[3]

    @pl.when(r == 0)
    def _():
        sign = jnp.where(
            lax.broadcasted_iota(jnp.int32, (tokens, head_dim), 1) < turn, -1.0, 1.0
        )
        base = base_ref[me]
        base_cos, base_sin = base[0:1], base[1:2]
        c, s = cos_ref[...], sin_ref[...]
        cos_s[...] = base_cos * c - base_sin * s
        sin_s[...] = (base_sin * c + base_cos * s) * sign
        stat_ref[...] = jnp.zeros_like(stat_ref)

    listed = list_ref[:, 0].reshape(steps * groups, slots).astype(jnp.float32).T
    block_ids = (
        lax.broadcasted_iota(jnp.int32, (blocks, groups * steps), 0) + me * blocks
    ).astype(jnp.float32)
    mask = jnp.full((blocks, groups * steps), NEG_FLOOR, jnp.float32)
    for j in range(slots):
        mask = jnp.where(listed[j : j + 1] == block_ids, 0.0, mask)
    bias_all = lax.dot_general(
        mask.astype(jnp.bfloat16), expand_ref[...], (((0,), (0,)), ((), ())),
        preferred_element_type=jnp.float32,
    )
    n_lists = groups * steps
    for c in range(tokens // head_dim):
        bias_s[c * n_lists : (c + 1) * n_lists] = bias_all[:, c * head_dim : (c + 1) * head_dim]

    count = n_heads + groups
    for t in range(steps):
        x = jnp.concatenate(
            [q_ref[t, 0].astype(jnp.float32), nk_ref[t, 0].astype(jnp.float32)], 0
        )
        head_s[t * count : (t + 1) * count] = (
            x * new_cos_ref[t : t + 1] + pltpu.roll(x, turn, 1) * new_sin_ref[t : t + 1]
        )
        nv_s[t * groups : (t + 1) * groups] = nv_ref[t, 0].astype(jnp.float32)

    def of_steps(ref, at, stride):
        return ref[pl.ds(at, steps, stride=stride)]

    cosine, sine = cos_s[...], sin_s[...]
    step_of = lax.broadcasted_iota(jnp.int32, (rows, steps), 0) % steps
    fresh_ok = (lax.broadcasted_iota(jnp.int32, (rows, steps), 1) <= step_of) & (me == 0)
    spot = lax.broadcasted_iota(jnp.int32, (part, lanes), 1) == (
        lax.broadcasted_iota(jnp.int32, (part, lanes), 0) + r * part
    )
    contract = (((1,), (1,)), ((), ()))
    zero = jnp.zeros((half, head_dim), jnp.bfloat16)
    keys_all = lax.dot_general(
        factor_ref[0], basis_ref[0], (((0,), (0,)), ((), ())), preferred_element_type=jnp.float32
    )
    for p in range(groups // 2):
        cols = slice(p * wide, (p + 1) * wide)
        keys = jnp.concatenate(
            [
                (k * cosine + pltpu.roll(k, turn, 1) * sine).astype(jnp.bfloat16)
                for k in (
                    keys_all[:, g * head_dim : (g + 1) * head_dim] for g in (2 * p, 2 * p + 1)
                )
            ],
            axis=1,
        )
        q = jnp.concatenate(
            [of_steps(head_s, h, count) for h in head_order[2 * p * group : 2 * (p + 1) * group]],
            0,
        ).astype(jnp.bfloat16)
        q = jnp.concatenate(
            [jnp.concatenate([q[:half], zero], 1), jnp.concatenate([zero, q[half:]], 1)], 0
        )
        nk = jnp.concatenate(
            [of_steps(head_s, n_heads + 2 * p + u, count) for u in range(2)], 1
        ).astype(jnp.bfloat16)
        nv = jnp.concatenate(
            [of_steps(nv_s, 2 * p + u, groups) for u in range(2)], 1
        ).astype(jnp.bfloat16)
        bias = jnp.concatenate(
            [
                jnp.concatenate(
                    [of_steps(bias_s, c * n_lists + 2 * p + u, groups) for u in range(2)], 0
                )
                for c in range(tokens // head_dim)
            ],
            1,
        )
        scores = lax.dot_general(q, keys, contract, preferred_element_type=jnp.float32) * scale
        scores = (
            scores.reshape(2, group, steps, tokens) + bias.reshape(2, 1, steps, tokens)
        ).reshape(rows, tokens)
        fresh = lax.dot_general(q, nk, contract, preferred_element_type=jnp.float32) * scale
        fresh = jnp.where(fresh_ok, fresh, NEG_FLOOR)
        top = jnp.maximum(
            jnp.max(scores, axis=1, keepdims=True), jnp.max(fresh, axis=1, keepdims=True)
        )
        weights = jnp.exp(scores - top)
        fresh = jnp.exp(fresh - top)
        total = jnp.sum(weights, axis=1, keepdims=True) + jnp.sum(fresh, axis=1, keepdims=True)

        def split_dot(w, v):
            high = w.astype(jnp.bfloat16)
            low = (w - high.astype(jnp.float32)).astype(jnp.bfloat16)
            both = jnp.dot(
                jnp.concatenate([high, low], 0), v, preferred_element_type=jnp.float32
            )
            return both[:rows] + both[rows:]

        out = split_dot(weights, value_ref[0, :, cols]) + split_dot(fresh, nv)
        for u in range(2):
            g = place[2 * p + u]
            mine = out[u * half : (u + 1) * half, u * head_dim : (u + 1) * head_dim]
            keep_ref[g, 0] = jnp.where(core == 0, mine[:part], mine[part:])
            send_ref[g, 0] = jnp.where(core == 0, mine[part:], mine[:part])
            for c in range(2):
                at = u * half + c * part
                for i, column in enumerate((top, total)):
                    stat_ref[c, i, g : g + 1] += jnp.sum(
                        jnp.where(spot, column[at : at + part], 0.0), axis=0, keepdims=True
                    )


def combine_kernel(
    chips, reqs, steps, send_ref, keep_ref, st_ref, w_ref, out_ref, w_s, o1, st1, weight_s, near,
    o2s, o2r, st2s, st2r, o3s, o3r, st3s, st3r, t1s, t1r, t2s, t2r, t3s, t3r, sem, k_sem, z_sem,
):
    me = lax.axis_index("store")
    chip, core = me // 2, me % 2
    lines = chips // 2
    line, side = chip // 2, chip % 2
    twin = chip * 2 + 1 - core
    mate = (line * 2 + 1 - side) * 2 + core
    rows = send_ref.shape[2]
    head_dim = send_ref.shape[3]
    heads = rows // (reqs * steps)
    width = out_ref.shape[1]

    weight_copy = pltpu.make_async_copy(w_ref, w_s, sem.at[0])
    weight_copy.start()

    def line_at(i):
        return lax.rem(line + i, lines)

    def device_of(z):
        return (z * 2 + side) * 2 + core

    def remote(src, dst, send, recv, device):
        return pltpu.make_async_remote_copy(
            src_ref=src, dst_ref=dst, send_sem=send, recv_sem=recv,
            device_id={"store": device}, device_id_type=MESH,
        )

    barrier = pltpu.get_barrier_semaphore()
    for device in (twin, mate):
        pl.semaphore_signal(barrier, inc=1, device_id={"store": device}, device_id_type=MESH)

    def greet(i, carry):
        pl.semaphore_signal(
            barrier, inc=1, device_id={"store": device_of(line_at(i))}, device_id_type=MESH
        )
        return carry

    lax.fori_loop(1, lines, greet, 0)
    pl.semaphore_wait(barrier, lines + 1)

    def loop(start, stop, step):
        def body(i, carry):
            step(line_at(i))
            return carry

        lax.fori_loop(start, stop, body, 0, unroll=lines <= 4)

    stats_1 = remote(st_ref.at[1 - core], st1, sem.at[1], sem.at[2], twin)
    stats_2 = remote(st2s, st2r, sem.at[3], sem.at[4], mate)

    def first(which):
        return remote(
            send_ref.at[which], o1.at[which], k_sem.at[0, which], k_sem.at[1, which], twin
        )

    def second(z):
        return remote(o2s.at[z], o2r.at[z], z_sem.at[0, z], z_sem.at[1, z], mate)

    def third(z, slot):
        device = device_of(z)
        return (
            remote(st3s.at[z], st3r.at[slot], z_sem.at[2, z], z_sem.at[3, slot], device),
            remote(o3s.at[z], o3r.at[slot], z_sem.at[4, z], z_sem.at[5, slot], device),
        )

    def twin_term(which, z):
        at = which * lines + z
        return remote(t1s.at[at], t1r.at[at], k_sem.at[2, at], k_sem.at[3, at], twin)

    def mate_term(z):
        return remote(t2s.at[z], t2r.at[z], z_sem.at[6, z], z_sem.at[7, z], mate)

    def line_term(z, slot):
        return remote(
            t3s.at[z], t3r.at[slot], z_sem.at[8, z], z_sem.at[9, slot], device_of(z)
        )

    other = 1 - side
    stats_1.start()
    first(other).start()
    first(side).start()

    def join(a_top, a_sum, b_top, b_sum):
        top = jnp.maximum(a_top, b_top)
        a, b = jnp.exp(a_top - top), jnp.exp(b_top - top)
        return top, a * a_sum + b * b_sum, a, b

    def spread(at, columns):
        columns = columns.T
        for k in range(columns.shape[1]):
            weight_s[at + k] = jnp.broadcast_to(columns[:, k : k + 1], (rows, head_dim))

    stats_1.wait_recv()
    my_top, my_sum, a, b = join(st_ref[core, 0], st_ref[core, 1], st1[0], st1[1])

    def side_of(x, which):
        return jnp.where(which == 0, x[:lines], x[lines:])

    st2s[0], st2s[1] = side_of(my_top, other), side_of(my_sum, other)
    stats_2.start()
    spread(0, jnp.concatenate([a, b], 0))

    def joined(which, z):
        k = which * lines + z
        return keep_ref[which, z] * weight_s[k] + o1[which, z] * weight_s[chips + k]

    first(other).wait_recv()

    def send_second(z):
        o2s[z] = joined(other, z).astype(jnp.bfloat16)
        second(z).start()

    loop(1, lines + 1, send_second)
    stats_2.wait_recv()
    near_top, near_sum, a, b = join(
        side_of(my_top, side), side_of(my_sum, side), st2r[0], st2r[1]
    )
    pad = jnp.zeros((6, rows), jnp.float32)
    for z in range(lines):
        st3s[z] = jnp.concatenate([near_top[z : z + 1], near_sum[z : z + 1], pad], 0)
    st3r[line] = st3s[line]
    loop(1, lines, lambda z: third(z, line)[0].start())
    first(side).wait_recv()
    for z in range(lines):
        near[z] = joined(side, z)
    spread(0, jnp.concatenate([a, b], 0))

    def paired(z):
        second(z).wait_recv()
        return near[z] * weight_s[z] + o2r[z].astype(jnp.float32) * weight_s[lines + z]

    def send_third(z):
        o3s[z] = paired(z).astype(jnp.bfloat16)
        third(z, line)[1].start()

    loop(1, lines, send_third)
    own = paired(line)
    loop(1, lines, lambda z: third(z, z)[0].wait_recv())
    tops = st3r[:, 0, :]
    share = jnp.exp(tops - jnp.max(tops, axis=0, keepdims=True))
    share = share / jnp.sum(share * st3r[:, 1, :], axis=0, keepdims=True)
    spread(0, share)

    def add_third(i, attn):
        z = line_at(i)
        third(z, z)[1].wait_recv()
        return attn + o3r[z].astype(jnp.float32) * weight_s[z]

    attn = lax.fori_loop(1, lines, add_third, own * weight_s[line], unroll=lines <= 4)
    flat = jnp.concatenate(
        [
            jnp.concatenate(
                [
                    attn[(r * heads + j) * steps : (r * heads + j + 1) * steps]
                    for r in range(reqs)
                ],
                0,
            )
            for j in range(heads)
        ],
        1,
    ).astype(jnp.bfloat16)
    weight_copy.wait()

    def term(which, z, half):
        at = pl.multiple_of(((2 * z + which) * 2 + half) * width, width)
        return jnp.dot(flat, w_s[:, pl.ds(at, width)], preferred_element_type=jnp.float32)

    def send_twin(which):
        def step(z):
            t1s[which * lines + z] = term(which, z, 1 - core)
            twin_term(which, z).start()

        loop(1, lines + 1, step)

    def twin_sum(which, z):
        mine = term(which, z, core)
        twin_term(which, z).wait_recv()
        return mine + t1r[which * lines + z]

    def send_mate(z):
        t2s[z] = twin_sum(other, z).astype(jnp.bfloat16)
        mate_term(z).start()

    def mate_sum(z):
        mine = twin_sum(side, z)
        mate_term(z).wait_recv()
        return mine + t2r[z].astype(jnp.float32)

    def send_line(z):
        t3s[z] = mate_sum(z).astype(jnp.bfloat16)
        line_term(z, line).start()

    send_twin(other)
    loop(1, lines + 1, send_mate)
    send_twin(side)
    loop(1, lines, send_line)
    own = mate_sum(line)

    def add_line(i, total):
        z = line_at(i)
        line_term(z, z).wait_recv()
        return total + t3r[z].astype(jnp.float32)

    out_ref[...] = lax.fori_loop(1, lines, add_line, own, unroll=lines <= 4).astype(out_ref.dtype)

    def drain(z):
        for copy in (second(z), twin_term(0, z), twin_term(1, z), mate_term(z)):
            copy.wait_send()

    def drain_lines(z):
        for copy in third(z, line) + (line_term(z, line),):
            copy.wait_send()

    loop(1, lines + 1, drain)
    loop(1, lines, drain_lines)
    for copy in (stats_1, stats_2, first(0), first(1)):
        copy.wait_send()


def per_device(
    queries, new_keys, new_values, key_factors, key_basis, values, block_index, block_count,
    out_weight,
):
    devices = lax.axis_size("store")
    chips = devices // 2
    steps, reqs, n_heads, head_dim = queries.shape
    groups = new_keys.shape[2]
    group = n_heads // groups
    tokens = values.shape[1]
    rank = key_factors.shape[2]
    blocks = tokens // BLOCK
    heads_dev = n_heads // devices
    slots = block_index.shape[-1]
    half_group = group // 2
    part = half_group * steps
    wide = groups * head_dim
    chips_group = half_group // heads_dev

    cos_off, sin_off = rope_tables(np.arange(tokens), head_dim)
    base = np.stack(rope_tables(np.arange(devices) * tokens, head_dim), 1)
    sign = np.where(np.arange(head_dim) < head_dim // 2, -1.0, 1.0).astype(np.float32)
    cos_new, sin_new = rope_tables(tokens * devices + np.arange(steps), head_dim)
    head_order = np.arange(n_heads).reshape(groups, chips_group, 2, heads_dev)
    head_order = tuple(int(h) for h in head_order.swapaxes(1, 2).reshape(-1))
    lines = chips // 2
    place = [g if chips_group > 1 else (g % 2) * lines + g // 2 for g in range(groups)]
    lists = jnp.where(
        jnp.arange(slots, dtype=jnp.int32) < block_count[..., None], block_index, -1
    )
    expand = (np.arange(tokens)[None, :] // BLOCK == np.arange(blocks)[:, None]).astype(
        jnp.bfloat16
    )

    def whole(shape):
        return pl.BlockSpec(shape, lambda r: (0,) * len(shape))

    def per_request(shape):
        return pl.BlockSpec((1,) + shape, lambda r: (r,) + (0,) * len(shape))

    def of_request(shape):
        return pl.BlockSpec((steps, 1) + shape, lambda r: (0, r) + (0,) * len(shape))

    lanes = reqs * part
    out_block = pl.BlockSpec((groups, 1, part, head_dim), lambda r: (0, r, 0, 0))
    send, keep, stats = pl.pallas_call(
        functools.partial(attend_kernel, steps, head_dim, head_order, place),
        grid=(reqs,),
        out_shape=(
            jax.ShapeDtypeStruct((groups, reqs, part, head_dim), jnp.float32),
            jax.ShapeDtypeStruct((groups, reqs, part, head_dim), jnp.float32),
            jax.ShapeDtypeStruct((2, 2, groups, lanes), jnp.float32),
        ),
        in_specs=[
            whole((devices, 2, head_dim)),
            whole((tokens, head_dim)),
            whole((tokens, head_dim)),
            whole((steps, head_dim)),
            whole((steps, head_dim)),
            whole((blocks, tokens)),
            of_request((n_heads, head_dim)),
            of_request((groups, head_dim)),
            of_request((groups, head_dim)),
            of_request((groups, slots)),
            per_request((rank, tokens)),
            per_request((rank, wide)),
            per_request((tokens, wide)),
        ],
        out_specs=(out_block, out_block, whole((2, 2, groups, lanes))),
        scratch_shapes=[
            pltpu.VMEM((tokens, head_dim), jnp.float32),
            pltpu.VMEM((tokens, head_dim), jnp.float32),
            pltpu.VMEM((steps * (n_heads + groups), head_dim), jnp.float32),
            pltpu.VMEM((steps * groups, head_dim), jnp.float32),
            pltpu.VMEM((steps * groups * tokens // head_dim, head_dim), jnp.float32),
        ],
        compiler_params=pltpu.CompilerParams(vmem_limit_bytes=60 * 2**20),
        name="attend",
    )(
        base, cos_off, sin_off, cos_new, sin_new * sign, expand, queries, new_keys, new_values,
        lists, key_factors.swapaxes(1, 2), key_basis, values,
    )
    rows_dev = reqs * heads_dev * steps

    def by_chip(y):
        if chips_group > 1:
            y = y.reshape(groups, reqs, chips_group, heads_dev * steps, head_dim)
            y = y.transpose(0, 2, 1, 3, 4).reshape(lines, 2, rows_dev, head_dim).swapaxes(0, 1)
        return y.reshape(2, lines, rows_dev, head_dim)

    if chips_group > 1:
        stats = stats.reshape(2, 2, groups, reqs, chips_group, heads_dev * steps)
        stats = stats.transpose(0, 1, 2, 4, 3, 5).reshape(2, 2, lines, 2, rows_dev)
        stats = stats.swapaxes(2, 3).reshape(2, 2, chips, rows_dev)

    width = out_weight.shape[1] // devices
    out_rows = reqs * steps
    dma = pltpu.SemaphoreType.DMA
    vmem = pl.BlockSpec(memory_space=pltpu.VMEM)
    out = pl.pallas_call(
        functools.partial(combine_kernel, chips, reqs, steps),
        out_shape=jax.ShapeDtypeStruct((out_rows, width), jnp.bfloat16),
        in_specs=[vmem, vmem, vmem, pl.BlockSpec(memory_space=pl.ANY)],
        out_specs=vmem,
        scratch_shapes=[
            pltpu.VMEM(out_weight.shape, out_weight.dtype),
            pltpu.VMEM((2, lines, rows_dev, head_dim), jnp.float32),
            pltpu.VMEM((2, chips, rows_dev), jnp.float32),
            pltpu.VMEM((2 * chips, rows_dev, head_dim), jnp.float32),
            pltpu.VMEM((lines, rows_dev, head_dim), jnp.float32),
            pltpu.VMEM((lines, rows_dev, head_dim), jnp.bfloat16),
            pltpu.VMEM((lines, rows_dev, head_dim), jnp.bfloat16),
            pltpu.VMEM((2, lines, rows_dev), jnp.float32),
            pltpu.VMEM((2, lines, rows_dev), jnp.float32),
            pltpu.VMEM((lines, rows_dev, head_dim), jnp.bfloat16),
            pltpu.VMEM((lines, rows_dev, head_dim), jnp.bfloat16),
            pltpu.VMEM((lines, 8, rows_dev), jnp.float32),
            pltpu.VMEM((lines, 8, rows_dev), jnp.float32),
            pltpu.VMEM((chips, out_rows, width), jnp.float32),
            pltpu.VMEM((chips, out_rows, width), jnp.float32),
        ]
        + [pltpu.VMEM((lines, out_rows, width), jnp.bfloat16)] * 4
        + [dma((5,)), dma((4, chips)), dma((10, lines))],
        compiler_params=pltpu.CompilerParams(
            collective_id=0, has_side_effects=True, vmem_limit_bytes=57 * 2**20
        ),
        name="combine",
    )(by_chip(send), by_chip(keep), stats, out_weight)
    return out.reshape(reqs, steps, width).transpose(1, 0, 2)


def solution(mesh):
    placed = (
        P(None, "parts", None, None),
        P(None, "parts", None, None),
        P(None, "parts", None, None),
        P("parts", "store", None),
        P("parts", None, None),
        P("parts", "store", None),
        P(None, "parts", None, None),
        P(None, "parts", None),
        P("store", None),
    )
    return jax.shard_map(
        per_device, mesh=mesh, in_specs=placed, out_specs=P(None, "parts", "store"), check_vma=False
    )
```

```python
import functools
import math

import jax
import jax.numpy as jnp
import numpy as np
from jax import lax
from jax.experimental import pallas as pl
from jax.experimental.pallas import tpu as pltpu
from jax.sharding import PartitionSpec as P

BLOCK = 8
ROPE_THETA = 500000.0
NEG_FLOOR = -1e30
MESH = pl.DeviceIdType.MESH


def rope_freqs(head_dim):
    exponent = np.arange(head_dim // 2, dtype=np.float64) * (2.0 / head_dim)
    base = np.power(ROPE_THETA, -exponent)
    wavelength = 2.0 * math.pi / base
    smooth = (8192.0 / wavelength - 1.0) / 3.0
    middle = (1.0 - smooth) * base / 8.0 + smooth * base
    freqs = np.where(wavelength < 2048.0, base, np.where(wavelength > 8192.0, base / 8.0, middle))
    return freqs.astype(np.float32).astype(np.float64)


def rope_tables(positions, head_dim):
    angles = positions[:, None].astype(np.float64) * rope_freqs(head_dim)[None, :]
    cosine, sine = np.cos(angles), np.sin(angles)
    return (
        np.concatenate([cosine, cosine], -1).astype(np.float32),
        np.concatenate([sine, sine], -1).astype(np.float32),
    )


def attend_kernel(
    steps, head_dim, head_order, place, base_ref, cos_ref, sin_ref, new_cos_ref, new_sin_ref,
    expand_ref, q_ref, nk_ref, nv_ref, list_ref, count_ref, factor_ref, basis_ref, value_ref, send_ref,
    keep_ref, stat_ref, cos_s, sin_s, head_s, nv_s, bias_s,
):
    r = pl.program_id(0)
    me = lax.axis_index("store")
    core = me % 2
    tokens = value_ref.shape[1]
    groups = value_ref.shape[2] // head_dim
    n_heads = q_ref.shape[2]
    group = n_heads // groups
    blocks = expand_ref.shape[0]
    slots = list_ref.shape[3]
    half = group * steps
    part = half // 2
    rows = 2 * half
    wide = 2 * head_dim
    turn = head_dim // 2
    scale = head_dim ** -0.5
    lanes = stat_ref.shape[3]

    @pl.when(r == 0)
    def _():
        sign = jnp.where(
            lax.broadcasted_iota(jnp.int32, (tokens, head_dim), 1) < turn, -1.0, 1.0
        )
        base = base_ref[me]
        base_cos, base_sin = base[0:1], base[1:2]
        c, s = cos_ref[...], sin_ref[...]
        cos_s[...] = base_cos * c - base_sin * s
        sin_s[...] = (base_sin * c + base_cos * s) * sign
        stat_ref[...] = jnp.zeros_like(stat_ref)

    listed = list_ref[:, 0].reshape(steps * groups, slots).astype(jnp.float32).T
    slot_ids = lax.broadcasted_iota(jnp.int32, (slots, steps * groups), 0)
    listed = jnp.where(slot_ids < count_ref[0], listed, -1.0)
    block_ids = (
        lax.broadcasted_iota(jnp.int32, (blocks, groups * steps), 0) + me * blocks
    ).astype(jnp.float32)
    mask = jnp.full((blocks, groups * steps), NEG_FLOOR, jnp.float32)
    for j in range(slots):
        mask = jnp.where(listed[j : j + 1] == block_ids, 0.0, mask)
    bias_all = lax.dot_general(
        mask.astype(jnp.bfloat16), expand_ref[...], (((0,), (0,)), ((), ())),
        preferred_element_type=jnp.float32,
    )
    n_lists = groups * steps
    for c in range(tokens // head_dim):
        bias_s[c * n_lists : (c + 1) * n_lists] = bias_all[:, c * head_dim : (c + 1) * head_dim]

    count = n_heads + groups
    for t in range(steps):
        x = jnp.concatenate(
            [q_ref[t, 0].astype(jnp.float32), nk_ref[t, 0].astype(jnp.float32)], 0
        )
        head_s[t * count : (t + 1) * count] = (
            x * new_cos_ref[t : t + 1] + pltpu.roll(x, turn, 1) * new_sin_ref[t : t + 1]
        )
        nv_s[t * groups : (t + 1) * groups] = nv_ref[t, 0].astype(jnp.float32)

    def of_steps(ref, at, stride):
        return ref[pl.ds(at, steps, stride=stride)]

    cosine, sine = cos_s[...], sin_s[...]
    step_of = lax.broadcasted_iota(jnp.int32, (rows, steps), 0) % steps
    fresh_ok = (lax.broadcasted_iota(jnp.int32, (rows, steps), 1) <= step_of) & (me == 0)
    spot = lax.broadcasted_iota(jnp.int32, (part, lanes), 1) == (
        lax.broadcasted_iota(jnp.int32, (part, lanes), 0) + r * part
    )
    contract = (((1,), (1,)), ((), ()))
    zero = jnp.zeros((half, head_dim), jnp.bfloat16)
    keys_all = lax.dot_general(
        factor_ref[0], basis_ref[0], (((0,), (0,)), ((), ())), preferred_element_type=jnp.float32
    )
    for p in range(groups // 2):
        cols = slice(p * wide, (p + 1) * wide)
        keys = jnp.concatenate(
            [
                (k * cosine + pltpu.roll(k, turn, 1) * sine).astype(jnp.bfloat16)
                for k in (
                    keys_all[:, g * head_dim : (g + 1) * head_dim] for g in (2 * p, 2 * p + 1)
                )
            ],
            axis=1,
        )
        q = jnp.concatenate(
            [of_steps(head_s, h, count) for h in head_order[2 * p * group : 2 * (p + 1) * group]],
            0,
        ).astype(jnp.bfloat16)
        q = jnp.concatenate(
            [jnp.concatenate([q[:half], zero], 1), jnp.concatenate([zero, q[half:]], 1)], 0
        )
        nk = jnp.concatenate(
            [of_steps(head_s, n_heads + 2 * p + u, count) for u in range(2)], 1
        ).astype(jnp.bfloat16)
        nv = jnp.concatenate(
            [of_steps(nv_s, 2 * p + u, groups) for u in range(2)], 1
        ).astype(jnp.bfloat16)
        bias = jnp.concatenate(
            [
                jnp.concatenate(
                    [of_steps(bias_s, c * n_lists + 2 * p + u, groups) for u in range(2)], 0
                )
                for c in range(tokens // head_dim)
            ],
            1,
        )
        scores = lax.dot_general(q, keys, contract, preferred_element_type=jnp.float32) * scale
        scores = (
            scores.reshape(2, group, steps, tokens) + bias.reshape(2, 1, steps, tokens)
        ).reshape(rows, tokens)
        fresh = lax.dot_general(q, nk, contract, preferred_element_type=jnp.float32) * scale
        fresh = jnp.where(fresh_ok, fresh, NEG_FLOOR)
        top = jnp.maximum(
            jnp.max(scores, axis=1, keepdims=True), jnp.max(fresh, axis=1, keepdims=True)
        )
        weights = jnp.exp(scores - top)
        fresh = jnp.exp(fresh - top)
        total = jnp.sum(weights, axis=1, keepdims=True) + jnp.sum(fresh, axis=1, keepdims=True)

        def split_dot(w, v):
            high = w.astype(jnp.bfloat16)
            low = (w - high.astype(jnp.float32)).astype(jnp.bfloat16)
            both = jnp.dot(
                jnp.concatenate([high, low], 0), v, preferred_element_type=jnp.float32
            )
            return both[:rows] + both[rows:]

        out = split_dot(weights, value_ref[0, :, cols]) + split_dot(fresh, nv)
        for u in range(2):
            g = place[2 * p + u]
            mine = out[u * half : (u + 1) * half, u * head_dim : (u + 1) * head_dim]
            keep_ref[g, 0] = jnp.where(core == 0, mine[:part], mine[part:])
            send_ref[g, 0] = jnp.where(core == 0, mine[part:], mine[:part])
            for c in range(2):
                at = u * half + c * part
                for i, column in enumerate((top, total)):
                    stat_ref[c, i, g : g + 1] += jnp.sum(
                        jnp.where(spot, column[at : at + part], 0.0), axis=0, keepdims=True
                    )


def combine_kernel(
    chips, reqs, steps, send_ref, keep_ref, st_ref, w_ref, out_ref, w_s, o1, st1, weight_s, near,
    o2s, o2r, st2s, st2r, o3s, o3r, st3s, st3r, t1s, t1r, t2s, t2r, t3s, t3r, sem, k_sem, z_sem,
):
    me = lax.axis_index("store")
    chip, core = me // 2, me % 2
    lines = chips // 2
    line, side = chip // 2, chip % 2
    twin = chip * 2 + 1 - core
    mate = (line * 2 + 1 - side) * 2 + core
    rows = send_ref.shape[2]
    head_dim = send_ref.shape[3]
    heads = rows // (reqs * steps)
    width = out_ref.shape[1]

    weight_copy = pltpu.make_async_copy(w_ref, w_s, sem.at[0])
    weight_copy.start()

    def line_at(i):
        return lax.rem(line + i, lines)

    def device_of(z):
        return (z * 2 + side) * 2 + core

    def remote(src, dst, send, recv, device):
        return pltpu.make_async_remote_copy(
            src_ref=src, dst_ref=dst, send_sem=send, recv_sem=recv,
            device_id={"store": device}, device_id_type=MESH,
        )

    barrier = pltpu.get_barrier_semaphore()
    for device in (twin, mate):
        pl.semaphore_signal(barrier, inc=1, device_id={"store": device}, device_id_type=MESH)

    def greet(i, carry):
        pl.semaphore_signal(
            barrier, inc=1, device_id={"store": device_of(line_at(i))}, device_id_type=MESH
        )
        return carry

    lax.fori_loop(1, lines, greet, 0)
    pl.semaphore_wait(barrier, lines + 1)

    def loop(start, stop, step):
        def body(i, carry):
            step(line_at(i))
            return carry

        lax.fori_loop(start, stop, body, 0, unroll=lines <= 4)

    stats_1 = remote(st_ref.at[1 - core], st1, sem.at[1], sem.at[2], twin)
    stats_2 = remote(st2s, st2r, sem.at[3], sem.at[4], mate)

    def first(which):
        return remote(
            send_ref.at[which], o1.at[which], k_sem.at[0, which], k_sem.at[1, which], twin
        )

    def second(z):
        return remote(o2s.at[z], o2r.at[z], z_sem.at[0, z], z_sem.at[1, z], mate)

    def third(z, slot):
        device = device_of(z)
        return (
            remote(st3s.at[z], st3r.at[slot], z_sem.at[2, z], z_sem.at[3, slot], device),
            remote(o3s.at[z], o3r.at[slot], z_sem.at[4, z], z_sem.at[5, slot], device),
        )

    def twin_term(which, z):
        at = which * lines + z
        return remote(t1s.at[at], t1r.at[at], k_sem.at[2, at], k_sem.at[3, at], twin)

    def mate_term(z):
        return remote(t2s.at[z], t2r.at[z], z_sem.at[6, z], z_sem.at[7, z], mate)

    def line_term(z, slot):
        return remote(
            t3s.at[z], t3r.at[slot], z_sem.at[8, z], z_sem.at[9, slot], device_of(z)
        )

    other = 1 - side
    stats_1.start()
    first(other).start()
    first(side).start()

    def join(a_top, a_sum, b_top, b_sum):
        top = jnp.maximum(a_top, b_top)
        a, b = jnp.exp(a_top - top), jnp.exp(b_top - top)
        return top, a * a_sum + b * b_sum, a, b

    def spread(at, columns):
        columns = columns.T
        for k in range(columns.shape[1]):
            weight_s[at + k] = jnp.broadcast_to(columns[:, k : k + 1], (rows, head_dim))

    stats_1.wait_recv()
    my_top, my_sum, a, b = join(st_ref[core, 0], st_ref[core, 1], st1[0], st1[1])

    def side_of(x, which):
        return jnp.where(which == 0, x[:lines], x[lines:])

    st2s[0], st2s[1] = side_of(my_top, other), side_of(my_sum, other)
    stats_2.start()
    spread(0, jnp.concatenate([a, b], 0))

    def joined(which, z):
        k = which * lines + z
        return keep_ref[which, z] * weight_s[k] + o1[which, z] * weight_s[chips + k]

    first(other).wait_recv()

    def send_second(z):
        o2s[z] = joined(other, z).astype(jnp.bfloat16)
        second(z).start()

    loop(1, lines + 1, send_second)
    stats_2.wait_recv()
    near_top, near_sum, a, b = join(
        side_of(my_top, side), side_of(my_sum, side), st2r[0], st2r[1]
    )
    pad = jnp.zeros((6, rows), jnp.float32)
    for z in range(lines):
        st3s[z] = jnp.concatenate([near_top[z : z + 1], near_sum[z : z + 1], pad], 0)
    st3r[line] = st3s[line]
    loop(1, lines, lambda z: third(z, line)[0].start())
    first(side).wait_recv()
    for z in range(lines):
        near[z] = joined(side, z)
    spread(0, jnp.concatenate([a, b], 0))

    def paired(z):
        second(z).wait_recv()
        return near[z] * weight_s[z] + o2r[z].astype(jnp.float32) * weight_s[lines + z]

    def send_third(z):
        o3s[z] = paired(z).astype(jnp.bfloat16)
        third(z, line)[1].start()

    loop(1, lines, send_third)
    own = paired(line)
    loop(1, lines, lambda z: third(z, z)[0].wait_recv())
    tops = st3r[:, 0, :]
    share = jnp.exp(tops - jnp.max(tops, axis=0, keepdims=True))
    share = share / jnp.sum(share * st3r[:, 1, :], axis=0, keepdims=True)
    spread(0, share)

    def add_third(i, attn):
        z = line_at(i)
        third(z, z)[1].wait_recv()
        return attn + o3r[z].astype(jnp.float32) * weight_s[z]

    attn = lax.fori_loop(1, lines, add_third, own * weight_s[line], unroll=lines <= 4)
    flat = jnp.concatenate(
        [
            jnp.concatenate(
                [
                    attn[(r * heads + j) * steps : (r * heads + j + 1) * steps]
                    for r in range(reqs)
                ],
                0,
            )
            for j in range(heads)
        ],
        1,
    ).astype(jnp.bfloat16)
    weight_copy.wait()

    def term(which, z, half):
        at = pl.multiple_of(((2 * z + which) * 2 + half) * width, width)
        return jnp.dot(flat, w_s[:, pl.ds(at, width)], preferred_element_type=jnp.float32)

    def send_twin(which):
        def step(z):
            t1s[which * lines + z] = term(which, z, 1 - core)
            twin_term(which, z).start()

        loop(1, lines + 1, step)

    def twin_sum(which, z):
        mine = term(which, z, core)
        twin_term(which, z).wait_recv()
        return mine + t1r[which * lines + z]

    def send_mate(z):
        t2s[z] = twin_sum(other, z).astype(jnp.bfloat16)
        mate_term(z).start()

    def mate_sum(z):
        mine = twin_sum(side, z)
        mate_term(z).wait_recv()
        return mine + t2r[z].astype(jnp.float32)

    def send_line(z):
        t3s[z] = mate_sum(z).astype(jnp.bfloat16)
        line_term(z, line).start()

    send_twin(other)
    loop(1, lines + 1, send_mate)
    send_twin(side)
    loop(1, lines, send_line)
    own = mate_sum(line)

    def add_line(i, total):
        z = line_at(i)
        line_term(z, z).wait_recv()
        return total + t3r[z].astype(jnp.float32)

    out_ref[...] = lax.fori_loop(1, lines, add_line, own, unroll=lines <= 4).astype(out_ref.dtype)

    def drain(z):
        for copy in (second(z), twin_term(0, z), twin_term(1, z), mate_term(z)):
            copy.wait_send()

    def drain_lines(z):
        for copy in third(z, line) + (line_term(z, line),):
            copy.wait_send()

    loop(1, lines + 1, drain)
    loop(1, lines, drain_lines)
    for copy in (stats_1, stats_2, first(0), first(1)):
        copy.wait_send()


def per_device(
    queries, new_keys, new_values, key_factors, key_basis, values, block_index, block_count,
    out_weight,
):
    devices = lax.axis_size("store")
    chips = devices // 2
    steps, reqs, n_heads, head_dim = queries.shape
    groups = new_keys.shape[2]
    group = n_heads // groups
    tokens = values.shape[1]
    rank = key_factors.shape[2]
    blocks = tokens // BLOCK
    heads_dev = n_heads // devices
    slots = block_index.shape[-1]
    half_group = group // 2
    part = half_group * steps
    wide = groups * head_dim
    chips_group = half_group // heads_dev

    cos_off, sin_off = rope_tables(np.arange(tokens), head_dim)
    base = np.stack(rope_tables(np.arange(devices) * tokens, head_dim), 1)
    sign = np.where(np.arange(head_dim) < head_dim // 2, -1.0, 1.0).astype(np.float32)
    cos_new, sin_new = rope_tables(tokens * devices + np.arange(steps), head_dim)
    head_order = np.arange(n_heads).reshape(groups, chips_group, 2, heads_dev)
    head_order = tuple(int(h) for h in head_order.swapaxes(1, 2).reshape(-1))
    lines = chips // 2
    place = [g if chips_group > 1 else (g % 2) * lines + g // 2 for g in range(groups)]
    counts = block_count.transpose(1, 0, 2).reshape(reqs, 1, steps * groups)
    expand = (np.arange(tokens)[None, :] // BLOCK == np.arange(blocks)[:, None]).astype(
        jnp.bfloat16
    )

    def whole(shape):
        return pl.BlockSpec(shape, lambda r: (0,) * len(shape))

    def per_request(shape):
        return pl.BlockSpec((1,) + shape, lambda r: (r,) + (0,) * len(shape))

    def of_request(shape):
        return pl.BlockSpec((steps, 1) + shape, lambda r: (0, r) + (0,) * len(shape))

    lanes = reqs * part
    out_block = pl.BlockSpec((groups, 1, part, head_dim), lambda r: (0, r, 0, 0))
    send, keep, stats = pl.pallas_call(
        functools.partial(attend_kernel, steps, head_dim, head_order, place),
        grid=(reqs,),
        out_shape=(
            jax.ShapeDtypeStruct((groups, reqs, part, head_dim), jnp.float32),
            jax.ShapeDtypeStruct((groups, reqs, part, head_dim), jnp.float32),
            jax.ShapeDtypeStruct((2, 2, groups, lanes), jnp.float32),
        ),
        in_specs=[
            whole((devices, 2, head_dim)),
            whole((tokens, head_dim)),
            whole((tokens, head_dim)),
            whole((steps, head_dim)),
            whole((steps, head_dim)),
            whole((blocks, tokens)),
            of_request((n_heads, head_dim)),
            of_request((groups, head_dim)),
            of_request((groups, head_dim)),
            of_request((groups, slots)),
            per_request((1, steps * groups)),
            per_request((rank, tokens)),
            per_request((rank, wide)),
            per_request((tokens, wide)),
        ],
        out_specs=(out_block, out_block, whole((2, 2, groups, lanes))),
        scratch_shapes=[
            pltpu.VMEM((tokens, head_dim), jnp.float32),
            pltpu.VMEM((tokens, head_dim), jnp.float32),
            pltpu.VMEM((steps * (n_heads + groups), head_dim), jnp.float32),
            pltpu.VMEM((steps * groups, head_dim), jnp.float32),
            pltpu.VMEM((steps * groups * tokens // head_dim, head_dim), jnp.float32),
        ],
        compiler_params=pltpu.CompilerParams(vmem_limit_bytes=60 * 2**20),
        name="attend",
    )(
        base, cos_off, sin_off, cos_new, sin_new * sign, expand, queries, new_keys, new_values,
        block_index, counts, key_factors.swapaxes(1, 2), key_basis, values,
    )
    rows_dev = reqs * heads_dev * steps

    def by_chip(y):
        if chips_group > 1:
            y = y.reshape(groups, reqs, chips_group, heads_dev * steps, head_dim)
            y = y.transpose(0, 2, 1, 3, 4).reshape(lines, 2, rows_dev, head_dim).swapaxes(0, 1)
        return y.reshape(2, lines, rows_dev, head_dim)

    if chips_group > 1:
        stats = stats.reshape(2, 2, groups, reqs, chips_group, heads_dev * steps)
        stats = stats.transpose(0, 1, 2, 4, 3, 5).reshape(2, 2, lines, 2, rows_dev)
        stats = stats.swapaxes(2, 3).reshape(2, 2, chips, rows_dev)

    width = out_weight.shape[1] // devices
    out_rows = reqs * steps
    dma = pltpu.SemaphoreType.DMA
    vmem = pl.BlockSpec(memory_space=pltpu.VMEM)
    out = pl.pallas_call(
        functools.partial(combine_kernel, chips, reqs, steps),
        out_shape=jax.ShapeDtypeStruct((out_rows, width), jnp.bfloat16),
        in_specs=[vmem, vmem, vmem, pl.BlockSpec(memory_space=pl.ANY)],
        out_specs=vmem,
        scratch_shapes=[
            pltpu.VMEM(out_weight.shape, out_weight.dtype),
            pltpu.VMEM((2, lines, rows_dev, head_dim), jnp.float32),
            pltpu.VMEM((2, chips, rows_dev), jnp.float32),
            pltpu.VMEM((2 * chips, rows_dev, head_dim), jnp.float32),
            pltpu.VMEM((lines, rows_dev, head_dim), jnp.float32),
            pltpu.VMEM((lines, rows_dev, head_dim), jnp.bfloat16),
            pltpu.VMEM((lines, rows_dev, head_dim), jnp.bfloat16),
            pltpu.VMEM((2, lines, rows_dev), jnp.float32),
            pltpu.VMEM((2, lines, rows_dev), jnp.float32),
            pltpu.VMEM((lines, rows_dev, head_dim), jnp.bfloat16),
            pltpu.VMEM((lines, rows_dev, head_dim), jnp.bfloat16),
            pltpu.VMEM((lines, 8, rows_dev), jnp.float32),
            pltpu.VMEM((lines, 8, rows_dev), jnp.float32),
            pltpu.VMEM((chips, out_rows, width), jnp.float32),
            pltpu.VMEM((chips, out_rows, width), jnp.float32),
        ]
        + [pltpu.VMEM((lines, out_rows, width), jnp.bfloat16)] * 4
        + [dma((5,)), dma((4, chips)), dma((10, lines))],
        compiler_params=pltpu.CompilerParams(
            collective_id=0, has_side_effects=True, vmem_limit_bytes=57 * 2**20
        ),
        name="combine",
    )(by_chip(send), by_chip(keep), stats, out_weight)
    return out.reshape(reqs, steps, width).transpose(1, 0, 2)


def solution(mesh):
    placed = (
        P(None, "parts", None, None),
        P(None, "parts", None, None),
        P(None, "parts", None, None),
        P("parts", "store", None),
        P("parts", None, None),
        P("parts", "store", None),
        P(None, "parts", None, None),
        P(None, "parts", None),
        P("store", None),
    )
    return jax.shard_map(
        per_device, mesh=mesh, in_specs=placed, out_specs=P(None, "parts", "store"), check_vma=False
    )
```
